32 devices in a mesh: dp: 16 (over z, x, core), tensor: 2 (over y).
Axes of the slice: x: 2, y: 2, z: 4, core: 2. Of those that a mesh axis runs over, the one named last changes fastest.
Arguments:
- hidden_in: bfloat16 [32768, 512], P(('dp', 'tensor')), may hold values from -6 to 6
- w_qkv: bfloat16 [3, 512, 512], P(None, None, 'tensor'), may hold values from -0.25 to 0.25
- qv_bias: float32 [2, 512], P(None, 'tensor'), may hold values from -3 to 3
- w_out: bfloat16 [512, 512], P('tensor'), may hold values from -1 to 1
- out_bias: float32 [512], replicated, may hold values from -3 to 3
- gain1: float32 [512], replicated, may hold values from 0.5 to 1.5
- shift1: float32 [512], replicated, may hold values from -3 to 3
- w_up: bfloat16 [512, 2048], P(None, 'tensor'), may hold values from -0.25 to 0.25
- up_bias: float32 [2048], P('tensor'), may hold values from -3 to 3
- w_down: bfloat16 [2048, 512], P('tensor'), may hold values from -0.125 to 0.125
- down_bias: float32 [512], replicated, may hold values from -3 to 3
- gain2: float32 [512], replicated, may hold values from 0.5 to 1.5
- shift2: float32 [512], replicated, may hold values from -3 to 3
- lengths: int32 [32], P('dp'), may hold values from 640 to 1024, as said below
- head_perm: int32 [8], P('tensor'), may hold values from 0 to 1
- cotangent: bfloat16 [32768, 512], P(('dp', 'tensor')), may hold values from -6 to 6
Outputs:
- out: bfloat16 [32768, 512], P(('dp', 'tensor'))
- x_grad: float32 [32768, 512], P(('dp', 'tensor'))
- w_qkv_grad: float32 [3, 512, 512], P(None, None, 'tensor')
- qv_bias_grad: float32 [2, 512], P(None, 'tensor')
- w_out_grad: float32 [512, 512], P('tensor')
- out_bias_grad: float32 [512], replicated
- gain1_grad: float32 [512], replicated
- shift1_grad: float32 [512], replicated
- w_up_grad: float32 [512, 2048], P(None, 'tensor')
- up_bias_grad: float32 [2048], P('tensor')
- w_down_grad: float32 [2048, 512], P('tensor')
- down_bias_grad: float32 [512], replicated
- gain2_grad: float32 [512], replicated
- shift2_grad: float32 [512], replicated
The draws below stay inside these ranges and needn't reach their ends.
Inputs may be any that keep to these rules, and one draw needn't show every extreme that they name: `lengths`: slots from a sequence's length up to 1024 are padding; some sequence has all 1024 slots real.
All inputs are finite; a program needn't handle non-finite values.
Results may differ from the reference program's by a relative error of at most 0.013.
The reference program's roundings to bfloat16 on the way count: a program that leaves them out, or rounds other values in their place, can miss the bound.
Values may be sent and summed in bfloat16 or wider, within the bound.
No kernel may reach another device: no remote copies, remote signals or barrier semaphores. Data moves between devices by JAX's collectives and lax.ppermute only.
A program may use at most 128 MiB of HBM per device.

```python
import math
import jax
import jax.numpy as jnp
from jax import lax

D = 512
HEADS = 8
HEAD_DIM = 64
FF = 2048
SEQ_LEN = 1024
SEQS = 32
TOKENS = 32768


def draw_lengths(key, part):
    least = SEQ_LEN // 2 + SEQ_LEN // 8
    base = jax.random.randint(jax.random.fold_in(key, 11), (SEQS,), least, SEQ_LEN + 1, dtype=jnp.int32)
    full_at = jax.random.randint(jax.random.fold_in(key, 12), (), 0, SEQS, dtype=jnp.int32)
    return jnp.where(jnp.arange(SEQS, dtype=jnp.int32) == full_at, SEQ_LEN, base).astype(jnp.int32)


def plant(entries, rng, low, top_value):
    shape = entries.shape
    index_at = [jax.random.randint(jax.random.fold_in(rng, axis), (), 0, shape[axis]) for axis in range(len(shape))]
    entries = entries.at[tuple(index_at)].set(low)
    longest = shape.index(max(shape))
    index_at[longest] = (index_at[longest] + 1) % shape[longest]
    return entries.at[tuple(index_at)].set(top_value)


def block_levels(key, extent, pieces, low, high):
    level, own = 1.0, jax.random.fold_in(key, 6)
    for dim, parts in pieces:
        steps = jnp.exp(jax.random.uniform(jax.random.fold_in(own, dim), (parts,), jnp.float32, low / len(pieces), high / len(pieces)))
        level = level * jnp.repeat(steps, extent[dim] // parts).reshape([-1 if axis == dim else 1 for axis in range(len(extent))])
    return level


def scatter_about(own_key, shape, width, reach, cuts=(), kind=jnp.bfloat16):
    entries = jax.random.normal(own_key, shape, jnp.float32) * width
    if len(cuts) > 0:
        entries = block_levels(own_key, shape, cuts, -0.22, 0.18) * entries
    return jnp.clip(entries, min=-reach, max=reach).astype(kind)


def setup_inputs(seed: int = 0) -> dict:
    key_list = jax.random.split(jax.random.key(seed), 17)
    return {
        "hidden_in": scatter_about(key_list[0], (TOKENS, D), 1.0, 6.0, ((0, 32),)),
        "w_qkv": scatter_about(key_list[1], (3, D, D), D ** -0.5, 0.25, ((2, 2),)),
        "qv_bias": scatter_about(key_list[2], (2, D), 0.5, 3.0, ((1, 2),), jnp.float32),
        "w_out": scatter_about(key_list[3], (D, D), (D // 16) ** -0.5, 1.0, ((0, 2),)),
        "out_bias": scatter_about(key_list[4], (D,), 0.5, 3.0, (), jnp.float32),
        "gain1": jnp.clip(1.0 + 0.1 * jax.random.normal(key_list[5], (D,), jnp.float32), 0.5, 1.5),
        "shift1": scatter_about(key_list[6], (D,), 0.5, 3.0, (), jnp.float32),
        "w_up": scatter_about(key_list[7], (D, FF), D ** -0.5, 0.25, ((1, 2),)),
        "up_bias": scatter_about(key_list[8], (FF,), 0.5, 3.0, ((0, 2),), jnp.float32),
        "w_down": scatter_about(key_list[9], (FF, D), FF ** -0.5, 0.125, ((0, 2),)),
        "down_bias": scatter_about(key_list[10], (D,), 0.5, 3.0, (), jnp.float32),
        "gain2": jnp.clip(1.0 + 0.1 * jax.random.normal(key_list[11], (D,), jnp.float32), 0.5, 1.5),
        "shift2": scatter_about(key_list[12], (D,), 0.5, 3.0, (), jnp.float32),
        "lengths": draw_lengths(jax.random.fold_in(key_list[16], 71), 0),
        "head_perm": plant(jax.random.randint(key_list[14], (HEADS,), 0, 2), jax.random.fold_in(key_list[14], 1), 0, 1).astype(jnp.int32),
        "cotangent": scatter_about(key_list[15], (TOKENS, D), 1.0, 6.0, ((0, 32),)),
    }


@jax.custom_vjp
def low(v):
    return lax.optimization_barrier(v.astype(jnp.bfloat16)).astype(jnp.float32)

@jax.custom_vjp
def low_back(v):
    return v

def low_keep(v):
    return (low(v), None)

def low_pass(kept, grad):
    return (grad,)

def back_keep(v):
    return (v, None)

def back_low(kept, grad):
    return (low(grad),)
low.defvjp(low_keep, low_pass)
low_back.defvjp(back_keep, back_low)
HIGHEST = lax.Precision.HIGHEST
EPSILON = 1e-05

def norm_rows(inputs, norm_gain, norm_shift):
    centre = inputs - lax.optimization_barrier(jnp.mean(inputs, axis=-1, keepdims=True))
    spread = lax.optimization_barrier(jnp.mean(centre * centre, axis=-1, keepdims=True))
    return centre * lax.rsqrt(spread + EPSILON) * norm_gain + norm_shift

def swap_halves(blocks, head_perm):
    flipped = jnp.flip(blocks, axis=1)
    chosen = (head_perm == 1).reshape((1, 1, 1, -1) + (1,) * (blocks.ndim - 4))
    return jnp.where(chosen, flipped, blocks)

def layer_forward(w_qkv, qv_bias, w_out, out_bias, gain1, shift1, w_up, up_bias, w_down, down_bias, gain2, shift2, rows_in, group_len, head_perm):
    groups = group_len.shape[0]
    half_len = SEQ_LEN // 2
    scaling = 1.0 / math.sqrt(HEAD_DIM)
    zero_bias = jnp.zeros_like(qv_bias[0])
    bias_all = jnp.stack([qv_bias[0], zero_bias, qv_bias[1]])
    projected = jnp.einsum('rd,cde->rce', rows_in, w_qkv, precision=HIGHEST) + bias_all[None]
    projected = low_back(low(projected))
    split_qkv = projected.reshape(groups, 2, half_len, 3, HEADS, HEAD_DIM)
    queries = split_qkv[:, :, :, 0]
    keys_perm = swap_halves(split_qkv[:, :, :, 1], head_perm)
    values_perm = swap_halves(split_qkv[:, :, :, 2], head_perm)
    positions = jnp.arange(SEQ_LEN, dtype=jnp.int32).reshape(1, 2, half_len)
    valid_pos = positions < group_len.reshape(groups, 1, 1)
    key_valid = swap_halves(jnp.broadcast_to(valid_pos[..., None], (groups, 2, half_len, HEADS)), head_perm)
    scores = jnp.einsum('giahd,gibhd->gihab', queries, keys_perm, precision=HIGHEST) * scaling
    scores = low_back(scores)
    allowed = jnp.transpose(key_valid, (0, 1, 3, 2))[:, :, :, None, :]
    scores = jnp.where(allowed, scores, -1e+30)
    row_max = lax.optimization_barrier(jnp.max(scores, axis=-1, keepdims=True))
    exponent = jnp.exp(scores - row_max)
    attn_probs = exponent / lax.optimization_barrier(jnp.sum(exponent, axis=-1, keepdims=True))
    context = jnp.einsum('gihab,gibhd->giahd', low(attn_probs), values_perm, precision=HIGHEST)
    context = low_back(low(context.reshape(groups * SEQ_LEN, D)))
    attn_out = jnp.dot(context, w_out, precision=HIGHEST) + out_bias
    normed1 = norm_rows(rows_in + low_back(attn_out), gain1, shift1)
    pre_act = low_back(jnp.dot(low(normed1), w_up, precision=HIGHEST) + up_bias)
    act_low = low(jax.nn.gelu(pre_act, approximate=False))
    ffn_out = jnp.dot(act_low, w_down, precision=HIGHEST) + down_bias
    normed2 = norm_rows(normed1 + low_back(ffn_out), gain2, shift2)
    row_valid = valid_pos.reshape(groups * SEQ_LEN, 1).astype(jnp.float32)
    return normed2 * row_valid

def reference(hidden_in, w_qkv, qv_bias, w_out, out_bias, gain1, shift1, w_up, up_bias, w_down, down_bias, gain2, shift2, lengths, head_perm, cotangent):
    group_seqs = math.gcd(SEQS, max(1, 4096 // SEQ_LEN))
    rounds = SEQS // group_seqs
    params = tuple((tensor_in.astype(jnp.float32) for tensor_in in (w_qkv, qv_bias, w_out, out_bias, gain1, shift1, w_up, up_bias, w_down, down_bias, gain2, shift2)))
    rows_groups = hidden_in.reshape(rounds, group_seqs * SEQ_LEN, D)
    cot_groups = cotangent.reshape(rounds, group_seqs * SEQ_LEN, D)
    len_groups = lengths.reshape(rounds, group_seqs)

    def one_round(totals, inputs):
        rows_part, cot_part, len_part = inputs

        def forward_fn(*arrays):
            return layer_forward(*arrays, len_part, head_perm)
        primal = params + (rows_part.astype(jnp.float32),)
        result, pullback = jax.vjp(forward_fn, *primal)
        grads = pullback(cot_part.astype(jnp.float32))
        totals = tuple((running + gradient for running, gradient in zip(totals, grads[:-1])))
        return (totals, (result.astype(jnp.bfloat16), grads[-1]))
    zeros_init = tuple((jnp.zeros_like(tensor_in) for tensor_in in params))
    totals, (outputs, x_grads) = lax.scan(one_round, zeros_init, (rows_groups, cot_groups, len_groups))
    out_rows = outputs.reshape(TOKENS, D)
    grad_rows = x_grads.reshape(TOKENS, D)
    return (out_rows, grad_rows, totals[0], totals[1], totals[2], totals[3], totals[4], totals[5], totals[6], totals[7], totals[8], totals[9], totals[10], totals[11])
```

```python
import math

import jax
import jax.numpy as jnp
from jax import lax
from jax.sharding import PartitionSpec as P

EPSILON = 1e-05
BF = jnp.bfloat16
F32 = jnp.float32


def ein(spec, a, b):
    return jnp.einsum(spec, a, b, preferred_element_type=F32)


def send_tensor(v):
    n = lax.axis_size("tensor")
    return jax.tree.map(lambda a: lax.ppermute(a, "tensor", [(i, (i + 1) % n) for i in range(n)]), v)


def send_bit(v, bit):
    n = lax.axis_size("dp")
    pairs = [(i, i ^ (1 << bit)) for i in range(n)]
    return jax.tree.map(lambda a: lax.ppermute(a, "dp", pairs), v)


def pick(a, axis, index):
    return lax.dynamic_index_in_dim(a, index, axis, keepdims=False)


def total_chips(buf):
    me = lax.axis_index("dp")
    bits = list(range(1, lax.axis_size("dp").bit_length() - 1))
    split, rest = bits[:3], bits[3:]
    for bit in split:
        side = (me >> bit) & 1
        half = buf.shape[0] // 2
        away = lax.dynamic_slice_in_dim(buf, (1 - side) * half, half, 0)
        kept = lax.dynamic_slice_in_dim(buf, side * half, half, 0)
        buf = (kept.astype(F32) + send_bit(away, bit).astype(F32)).astype(BF)
    for bit in rest:
        buf = (buf.astype(F32) + send_bit(buf, bit).astype(F32)).astype(BF)
    for bit in reversed(split):
        side = (me >> bit) & 1
        got = send_bit(buf, bit)
        first = jnp.where(side == 0, buf, got)
        second = jnp.where(side == 0, got, buf)
        buf = jnp.concatenate([first, second], axis=0)
    return buf


def norm_parts(v):
    centre = v - jnp.mean(v, axis=-1, keepdims=True)
    spread = jnp.mean(centre * centre, axis=-1, keepdims=True)
    inv = lax.rsqrt(spread + EPSILON)
    return centre * inv, inv


def norm_back(g, hat, inv, gain):
    gg = g * gain
    mean_g = jnp.mean(gg, axis=-1, keepdims=True)
    mean_gh = jnp.mean(gg * hat, axis=-1, keepdims=True)
    return (gg - mean_g - hat * mean_gh) * inv


def local(hidden_in, w_qkv, qv_bias, w_out, out_bias, gain1, shift1, w_up, up_bias, w_down,
          down_bias, gain2, shift2, lengths, head_perm, cotangent):
    rows, width = hidden_in.shape
    half = rows // 2
    core = lax.axis_index("dp") % 2
    length = lengths[lax.axis_index("tensor")]
    valid = jnp.arange(rows, dtype=jnp.int32) < length
    row_valid = valid.astype(F32)[:, None]
    pair = w_qkv.shape[2] // 2
    heads = head_perm.shape[0] // 2
    size = pair // heads
    units = up_bias.shape[0] // 2

    def slot(i):
        small = jnp.concatenate([
            pick(qv_bias.reshape(2, 2, pair), 1, i).reshape(-1),
            pick(up_bias.reshape(2, units), 0, i),
            pick(head_perm.reshape(2, heads), 0, i).astype(F32)])
        return (pick(w_qkv.reshape(3, width, 2, pair), 2, i), small,
                pick(w_out.reshape(2, pair, width), 0, i),
                pick(w_up.reshape(width, 2, units), 1, i),
                pick(w_down.reshape(2, units, width), 0, i))

    own_m = slot(core)
    own_p = slot(1 - core)
    other_m = send_tensor(own_m)
    other_p = send_bit(other_m, 0)
    slots = [own_m, own_p, other_m, other_p]

    def flip(a, perm):
        chosen = (perm == 1).reshape((1, 1, heads) + (1,) * (a.ndim - 3))
        return jnp.where(chosen, a[::-1], a)

    scaling = 1.0 / math.sqrt(size)
    kept = []
    attn = 0.0
    for wq, small, wo, _, _ in slots:
        bias = small[: 2 * pair].reshape(2, pair)
        perm = small[2 * pair + units:]
        bias3 = jnp.stack([bias[0], jnp.zeros_like(bias[0]), bias[1]])
        qkv = (ein("rd,cde->cre", hidden_in, wq) + bias3[:, None]).astype(BF)
        qkv = qkv.reshape(3, 2, half, heads, size)
        q, k, v = qkv[0], flip(qkv[1], perm), flip(qkv[2], perm)
        ok = flip(jnp.broadcast_to(valid.reshape(2, half, 1), (2, half, heads)), perm)
        s = ein("iahd,ibhd->ihab", q, k) * scaling
        s = jnp.where(jnp.transpose(ok, (0, 2, 1))[:, :, None, :], s, -1e30)
        m = jnp.max(s, axis=-1, keepdims=True)
        e = jnp.exp(s - m)
        p = e / jnp.sum(e, axis=-1, keepdims=True)
        p_low = p.astype(BF)
        ctx = ein("ihab,ibhd->iahd", p_low, v)
        ctx = ctx.astype(BF).reshape(rows, pair)
        kept.append((q, k, v, p_low, ctx, perm))
        attn = attn + jnp.dot(ctx, wo, preferred_element_type=F32)

    z1 = hidden_in.astype(F32) + attn + out_bias
    hat1, inv1 = norm_parts(z1)
    n1 = hat1 * gain1 + shift1
    n1_low = n1.astype(BF)
    ffn = 0.0
    pres = []
    for _, small, _, wu, wd in slots:
        pre = jnp.dot(n1_low, wu, preferred_element_type=F32) + small[2 * pair: 2 * pair + units]
        cdf = 0.5 * (1.0 + lax.erf(pre * math.sqrt(0.5)))
        act = (pre * cdf).astype(BF)
        slope = cdf + pre * jnp.exp(-0.5 * pre * pre) * (1.0 / math.sqrt(2.0 * math.pi))
        pres.append((act, slope))
        ffn = ffn + jnp.dot(act, wd, preferred_element_type=F32)
    z2 = n1 + ffn + down_bias
    hat2, inv2 = norm_parts(z2)
    out = ((hat2 * gain2 + shift2) * row_valid).astype(BF)
    g_out = cotangent.astype(F32) * row_valid
    d_gain2 = jnp.sum(g_out * hat2, axis=0)
    d_shift2 = jnp.sum(g_out, axis=0)
    g_z2 = norm_back(g_out, hat2, inv2, gain2)
    g_ffn = g_z2.astype(BF)
    d_down_bias = jnp.sum(g_ffn, axis=0, dtype=F32)
    g_n1 = g_z2
    d_ffn = []
    for (_, _, _, wu, wd), (act, slope) in zip(slots, pres):
        d_wd = ein("rf,rd->fd", act, g_ffn)
        g_pre = (ein("rd,fd->rf", g_ffn, wd) * slope).astype(BF)
        d_ub = jnp.sum(g_pre, axis=0, dtype=F32)
        d_wu = ein("rd,rf->df", n1_low, g_pre)
        g_n1 = g_n1 + ein("rf,df->rd", g_pre, wu)
        d_ffn.append((d_wu, d_ub, d_wd))
    d_gain1 = jnp.sum(g_n1 * hat1, axis=0)
    d_shift1 = jnp.sum(g_n1, axis=0)
    g_z1 = norm_back(g_n1, hat1, inv1, gain1)
    g_attn = g_z1.astype(BF)
    d_out_bias = jnp.sum(g_attn, axis=0, dtype=F32)
    x_grad = g_z1
    d_attn = []
    for (wq, _, wo, _, _), (q, k, v, p_low, ctx, perm) in zip(slots, kept):
        d_wo = ein("rc,rd->cd", ctx, g_attn)
        g_ctx = ein("rd,cd->rc", g_attn, wo).astype(BF).reshape(2, half, heads, size)
        dv = flip(ein("ihab,iahd->ibhd", p_low, g_ctx), perm)
        dp = ein("iahd,ibhd->ihab", g_ctx, v)
        p = p_low.astype(F32)
        ds = (p * (dp - jnp.sum(p * dp, axis=-1, keepdims=True))).astype(BF)
        dq = ein("ihab,ibhd->iahd", ds, k) * scaling
        dk = flip(ein("ihab,iahd->ibhd", ds, q) * scaling, perm)
        g_qkv = jnp.stack([dq, dk, dv]).astype(BF).reshape(3, rows, pair)
        sums = jnp.sum(g_qkv, axis=1, dtype=F32)
        d_wq = ein("rd,cre->cde", hidden_in, g_qkv)
        x_grad = x_grad + ein("cre,cde->rd", g_qkv, wq)
        d_attn.append((d_wq, jnp.stack([sums[0], sums[2]]), d_wo))

    common = jnp.stack([d_out_bias, d_gain1, d_shift1, d_down_bias, d_gain2, d_shift2]).astype(BF)

    def flat(i):
        d_wu, d_ub, d_wd = d_ffn[i]
        d_wq, d_b, d_wo = d_attn[i]
        return [d_wu.astype(BF), d_wd.astype(BF), d_wq.astype(BF), d_wo.astype(BF), d_ub.astype(BF), d_b.astype(BF)]

    def plus(a, b):
        return jax.tree.map(lambda u, v: (u.astype(F32) + v.astype(F32)).astype(BF), a, b)

    got = send_bit((flat(1), flat(3), common), 0)
    own, other, common = plus((flat(0), flat(2), common), got)
    own, common = plus((own, common), send_tensor((other, common)))
    parts = own + [common]
    shapes = [a.shape for a in parts]
    line = jnp.concatenate([a.reshape(-1) for a in parts])
    unit = 512 * 8 * 16
    pad = -line.size % unit
    line = jnp.pad(line, (0, pad)).reshape(-1, 512)
    line = total_chips(line)
    mate = send_bit(line, 0)
    both = [line, mate]
    first = jnp.where(core == 0, line, mate).reshape(-1)
    second = jnp.where(core == 0, mate, line).reshape(-1)

    def unpack(v):
        out, at = [], 0
        for s in shapes:
            n = math.prod(s)
            out.append(v[at: at + n].reshape(s).astype(F32))
            at += n
        return out

    a, b = unpack(first), unpack(second)
    d_wu = jnp.concatenate([a[0], b[0]], axis=1)
    d_wd = jnp.concatenate([a[1], b[1]], axis=0)
    d_wq = jnp.concatenate([a[2], b[2]], axis=2)
    d_wo = jnp.concatenate([a[3], b[3]], axis=0)
    d_ub = jnp.concatenate([a[4], b[4]], axis=0)
    d_qvb = jnp.concatenate([a[5], b[5]], axis=1)
    com = a[6]
    return (out, x_grad, d_wq, d_qvb, d_wo, com[0], com[1], com[2], d_wu, d_ub, d_wd, com[3], com[4], com[5])


def solution(mesh):
    whole = P()
    rows = P(("dp", "tensor"), None)
    return jax.shard_map(
        local,
        mesh=mesh,
        in_specs=(rows, P(None, None, "tensor"), P(None, "tensor"), P("tensor", None), whole, whole, whole,
                  P(None, "tensor"), P("tensor"), P("tensor", None), whole, whole, whole, P("dp"), P("tensor"), rows),
        out_specs=(rows, rows, P(None, None, "tensor"), P(None, "tensor"), P("tensor", None), whole, whole, whole,
                   P(None, "tensor"), P("tensor"), P("tensor", None), whole, whole, whole),
        check_vma=False,
    )
```

```python
import math
from functools import partial
import jax
import jax.numpy as jnp
from jax import lax
from jax.experimental import pallas as pl
from jax.experimental.pallas import tpu as pltpu
from jax.sharding import PartitionSpec as P

EPSILON = 1e-05
BF = jnp.bfloat16
F32 = jnp.float32
VMEM_BYTES = 56 * 1024 * 1024


def dot(a, b, ca, cb):
    return lax.dot_general(a, b, (((ca,), (cb,)), ((), ())), preferred_element_type=F32)


def forward_kernel(scalars, x_ref, w_ref, bias_ref, qkv_ref, e_ref, inv_ref, ctx_ref):
    width, rows = qkv_ref.shape[1:]
    half = rows // 2
    heads = e_ref.shape[1]
    size = width // heads
    i = pl.program_id(0)

    @pl.when(i == 0)
    def _():
        for c in range(3):
            part = dot(w_ref[c], x_ref[...], 0, 1)
            if c != 1:
                part = part + bias_ref[c // 2]
            qkv_ref[c] = part.astype(BF)

    length = scalars[1]
    mine = pl.ds(pl.multiple_of(i * half, half), half)
    factor = math.log2(math.e) / math.sqrt(size)
    for h in range(heads):
        lanes = slice(h * size, (h + 1) * size)
        j = i ^ scalars[2 + h]
        theirs = pl.ds(pl.multiple_of(j * half, half), half)
        s = dot(qkv_ref[1, lanes, theirs], qkv_ref[0, lanes, mine], 0, 0)
        key = lax.broadcasted_iota(jnp.int32, (half, 1), 0) + j * half
        s = jnp.where(key < length, s, -1e30)
        top = jnp.max(s, axis=0, keepdims=True)
        e = jnp.exp2((s - top) * factor)
        inv = 1.0 / jnp.sum(e, axis=0, keepdims=True)
        low = e.astype(BF)
        e_ref[0, h] = low
        inv_ref[0, h] = inv
        ctx = dot(qkv_ref[2, lanes, theirs], low, 1, 0) * inv
        ctx_ref[lanes, mine] = ctx.astype(BF)


def attend_forward(x, w, bias, scalars):
    rows, width = x.shape
    heads = scalars.shape[0] - 2
    pair = bias.shape[1]
    half = rows // 2
    once = lambda *shape: pl.BlockSpec(shape, lambda i, s: (0,) * len(shape))
    return pl.pallas_call(
        forward_kernel,
        out_shape=(
            jax.ShapeDtypeStruct((3, pair, rows), BF),
            jax.ShapeDtypeStruct((2, heads, half, half), BF),
            jax.ShapeDtypeStruct((2, heads, 1, half), F32),
            jax.ShapeDtypeStruct((pair, rows), BF),
        ),
        grid_spec=pltpu.PrefetchScalarGridSpec(
            num_scalar_prefetch=1,
            grid=(2,),
            in_specs=[
                once(rows, width),
                pl.BlockSpec((3, width, pair), lambda i, s: (0, 0, s[0])),
                once(2, pair, 1),
            ],
            out_specs=(
                once(3, pair, rows),
                pl.BlockSpec((1, heads, half, half), lambda i, s: (i, 0, 0, 0)),
                pl.BlockSpec((1, heads, 1, half), lambda i, s: (i, 0, 0, 0)),
                once(pair, rows),
            ),
        ),
        compiler_params=pltpu.CompilerParams(vmem_limit_bytes=VMEM_BYTES),
        cost_estimate=pl.CostEstimate(flops=2_000_000_000, bytes_accessed=5_000_000, transcendentals=1_000_000),
        name="attend_forward",
    )(scalars, x, w, bias)


def backward_kernel(scalars, x_ref, wo_ref, qkv_ref, e_ref, inv_ref, ctx_ref, ga_ref,
                    g_ref, dw_ref, sums_ref, gc_ref):
    width, rows = gc_ref.shape
    half = rows // 2
    heads = e_ref.shape[1]
    size = width // heads
    i = pl.program_id(0)

    @pl.when(i == 0)
    def _():
        gc_ref[...] = dot(wo_ref[...], ga_ref[...], 1, 1).astype(BF)
        dw_ref[3 * width:] = dot(ctx_ref[...], ga_ref[...], 1, 0).astype(BF)

    mine = pl.ds(pl.multiple_of(i * half, half), half)
    scaling = 1.0 / math.sqrt(size)
    for h in range(heads):
        lanes = slice(h * size, (h + 1) * size)
        j = i ^ scalars[2 + h]
        theirs = pl.ds(pl.multiple_of(j * half, half), half)
        g = gc_ref[lanes, mine].astype(F32) * inv_ref[0, h]
        inner = jnp.sum(g * ctx_ref[lanes, mine].astype(F32), axis=0, keepdims=True)
        g = g.astype(BF)
        e = e_ref[0, h]
        dp = dot(qkv_ref[2, lanes, theirs], g, 0, 0)
        ds = (e.astype(F32) * (dp - inner)).astype(BF)
        g_ref[2, lanes, theirs] = dot(g, e, 1, 1).astype(BF)
        g_ref[1, lanes, theirs] = (dot(qkv_ref[0, lanes, mine], ds, 1, 1) * scaling).astype(BF)
        g_ref[0, lanes, mine] = (dot(qkv_ref[1, lanes, theirs], ds, 1, 0) * scaling).astype(BF)

    @pl.when(i == 1)
    def _():
        for c in range(3):
            dw_ref[c * width: (c + 1) * width] = dot(g_ref[c], x_ref[...], 1, 0).astype(BF)
            if c != 1:
                sums_ref[c // 2] = jnp.sum(g_ref[c].astype(F32), axis=1, keepdims=True)


def attend_backward(x, wo, qkv, e, inv, ctx, g_attn, scalars):
    rows, width = x.shape
    heads = e.shape[1]
    pair = ctx.shape[0]
    half = rows // 2
    once = lambda *shape: pl.BlockSpec(shape, lambda i, s: (0,) * len(shape))
    return pl.pallas_call(
        backward_kernel,
        out_shape=(
            jax.ShapeDtypeStruct((3, pair, rows), BF),
            jax.ShapeDtypeStruct((4 * pair, width), BF),
            jax.ShapeDtypeStruct((2, pair, 1), F32),
        ),
        grid_spec=pltpu.PrefetchScalarGridSpec(
            num_scalar_prefetch=1,
            grid=(2,),
            in_specs=[
                once(rows, width),
                pl.BlockSpec((pair, width), lambda i, s: (s[0], 0)),
                once(3, pair, rows),
                pl.BlockSpec((1, heads, half, half), lambda i, s: (i, 0, 0, 0)),
                pl.BlockSpec((1, heads, 1, half), lambda i, s: (i, 0, 0, 0)),
                once(pair, rows),
                once(rows, width),
            ],
            out_specs=(once(3, pair, rows), once(4 * pair, width), once(2, pair, 1)),
            scratch_shapes=[pltpu.VMEM((pair, rows), BF)],
        ),
        compiler_params=pltpu.CompilerParams(vmem_limit_bytes=VMEM_BYTES),
        cost_estimate=pl.CostEstimate(flops=4_000_000_000, bytes_accessed=6_000_000, transcendentals=0),
        name="attend_backward",
    )(scalars, x, wo, qkv, e, inv, ctx, g_attn)


def normed(v):
    centre = v - jnp.mean(v, axis=-1, keepdims=True)
    inv = lax.rsqrt(jnp.mean(centre * centre, axis=-1, keepdims=True) + EPSILON)
    return centre * inv, inv


def norm_back(g, hat, inv, gain):
    g = g * gain
    return (g - jnp.mean(g, axis=-1, keepdims=True) - hat * jnp.mean(g * hat, axis=-1, keepdims=True)) * inv


def gelu_parts(v):
    t = 1.0 / (1.0 + (0.3275911 * math.sqrt(0.5)) * jnp.abs(v))
    bell = jnp.exp2(v * v * (-0.5 * math.log2(math.e)))
    poly = ((((0.5 * 1.061405429 * t - 0.5 * 1.453152027) * t + 0.5 * 1.421413741) * t
             - 0.5 * 0.284496736) * t + 0.5 * 0.254829592) * t
    tail = poly * bell
    cdf = jnp.where(v < 0, tail, 1.0 - tail)
    return v * cdf, cdf + v * bell * (1.0 / math.sqrt(2.0 * math.pi))


def dense_kernel(scalars, x_ref, cot_ref, c0, c1, c2, c3, vec_ref, wo_own, wu_own, wd_own, ub_own, ub_m, ub_p,
                 pack_m, pack_p, out_ref, gz_ref, ga_ref, gm_ref, gp_ref, dub_ref, common_ref,
                 wo_all, n1_all, gf_all, act_all, gp_all, tile):
    rows, width = x_ref.shape
    pair = c0.shape[0]
    units = ub_m.shape[1]
    core, length = scalars[0], scalars[1]

    def at(i, n):
        return pl.ds(pl.multiple_of((core ^ i) * n, n), n)

    wo_all[0:pair] = wo_own[at(0, pair)]
    wo_all[pair: 2 * pair] = wo_own[at(1, pair)]
    wo_all[2 * pair: 3 * pair] = pack_m[2 * units:]
    wo_all[3 * pair:] = pack_p[2 * units:]
    ups = [wu_own.at[:, at(0, units)], wu_own.at[:, at(1, units)], pack_m.at[:units], pack_p.at[:units]]
    downs = [wd_own.at[at(0, units)], wd_own.at[at(1, units)], pack_m.at[units: 2 * units], pack_p.at[units: 2 * units]]
    biases = [ub_own.at[:, at(0, units)], ub_own.at[:, at(1, units)], ub_m, ub_p]
    out_bias, gain1, shift1, down_bias, gain2, shift2 = (vec_ref[k: k + 1] for k in range(6))
    dub_ref[...] = jnp.zeros_like(dub_ref)
    common_ref[...] = jnp.zeros_like(common_ref)

    @pl.loop(0, rows // tile)
    def _(r):
        here = pl.ds(pl.multiple_of(r * tile, tile), tile)
        ctx = jnp.concatenate([c[:, here] for c in (c0, c1, c2, c3)], axis=0)
        z1 = x_ref[here].astype(F32) + dot(ctx, wo_all[...], 0, 0) + out_bias
        hat1, inv1 = normed(z1)
        n1 = hat1 * gain1 + shift1
        low = n1.astype(BF)
        n1_all[here] = low
        z2 = n1 + down_bias
        for k in range(4):
            cols = slice(k * units, (k + 1) * units)
            act, slope = gelu_parts(dot(low, ups[k][...], 1, 0) + biases[k][...])
            act = act.astype(BF)
            act_all[here, cols] = act
            gp_all[here, cols] = slope.astype(BF)
            z2 = z2 + dot(act, downs[k][...], 1, 0)
        hat2, inv2 = normed(z2)
        row = lax.broadcasted_iota(jnp.int32, (tile, 1), 0) + r * tile
        valid = (row < length).astype(F32)
        out_ref[here] = ((hat2 * gain2 + shift2) * valid).astype(BF)
        g_out = cot_ref[here].astype(F32) * valid
        g_z2 = norm_back(g_out, hat2, inv2, gain2)
        g_ffn = g_z2.astype(BF)
        gf_all[here] = g_ffn
        g_n1 = g_z2
        for k in range(4):
            cols = slice(k * units, (k + 1) * units)
            g_pre = (dot(g_ffn, downs[k][...], 1, 1) * gp_all[here, cols].astype(F32)).astype(BF)
            gp_all[here, cols] = g_pre
            dub_ref[k: k + 1] += jnp.sum(g_pre.astype(F32), axis=0, keepdims=True)
            g_n1 = g_n1 + dot(g_pre, ups[k][...], 1, 1)
        g_z1 = norm_back(g_n1, hat1, inv1, gain1)
        gz_ref[here] = g_z1
        g_attn = g_z1.astype(BF)
        ga_ref[here] = g_attn
        sums = (g_attn.astype(F32), g_n1 * hat1, g_n1, g_ffn.astype(F32), g_out * hat2, g_out)
        for k, v in enumerate(sums):
            common_ref[k: k + 1] += jnp.sum(v, axis=0, keepdims=True)

    flipped = n1_all[...].T
    for k in range(4):
        cols = slice(k * units, (k + 1) * units)
        to = (gm_ref, gp_ref)[k % 2].at[k // 2]
        to[:width] = dot(flipped, gp_all[:, cols], 1, 0).astype(BF)
        to[width:] = dot(act_all[:, cols], gf_all[...], 0, 0).astype(BF)


def dense(scalars, x, cot, ctxs, vec, wo, wu, wd, biases, packs):
    rows, width = x.shape
    pair = ctxs[0].shape[0]
    units = biases[1].shape[1]
    tile = 256
    args = [x, cot, *ctxs, vec, wo, wu, wd, *biases, *packs]
    whole = lambda a: pl.BlockSpec(a.shape, lambda i, s: (0,) * len(a.shape))
    outs = (
        jax.ShapeDtypeStruct((rows, width), BF),
        jax.ShapeDtypeStruct((rows, width), F32),
        jax.ShapeDtypeStruct((rows, width), BF),
        jax.ShapeDtypeStruct((2, width + units, width), BF),
        jax.ShapeDtypeStruct((2, width + units, width), BF),
        jax.ShapeDtypeStruct((4, units), F32),
        jax.ShapeDtypeStruct((6, width), F32),
    )
    return pl.pallas_call(
        partial(dense_kernel, tile=tile),
        out_shape=outs,
        grid_spec=pltpu.PrefetchScalarGridSpec(
            num_scalar_prefetch=1,
            grid=(1,),
            in_specs=[whole(a) for a in args],
            out_specs=tuple(whole(a) for a in outs),
            scratch_shapes=[
                pltpu.VMEM((4 * pair, width), BF),
                pltpu.VMEM((rows, width), BF),
                pltpu.VMEM((rows, width), BF),
                pltpu.VMEM((rows, 4 * units), BF),
                pltpu.VMEM((rows, 4 * units), BF),
            ],
        ),
        compiler_params=pltpu.CompilerParams(vmem_limit_bytes=VMEM_BYTES),
        cost_estimate=pl.CostEstimate(flops=14_000_000_000, bytes_accessed=20_000_000, transcendentals=4_000_000),
        name="dense",
    )(scalars, *args)


def input_kernel(scalars, gz_ref, w_own, w_m, w_p, g0, g1, g2, g3, out_ref, tile):
    rows, width = gz_ref.shape
    pair = g0.shape[1]
    core = scalars[0]
    spots = [pl.ds(pl.multiple_of((core ^ i) * pair, pair), pair) for i in range(2)]

    @pl.loop(0, rows // tile)
    def _(r):
        here = pl.ds(pl.multiple_of(r * tile, tile), tile)
        total = gz_ref[here]
        for c in range(3):
            g = jnp.concatenate([g0[c, :, here], g1[c, :, here], g2[c, :, here], g3[c, :, here]], axis=0)
            w = jnp.concatenate([w_own[c, :, spots[0]], w_own[c, :, spots[1]], w_m[c], w_p[c]], axis=1)
            total = total + dot(g, w, 0, 1)
        out_ref[here] = total


def input_gradient(scalars, gz, w_own, w_m, w_p, gs):
    args = [gz, w_own, w_m, w_p, *gs]
    whole = lambda a: pl.BlockSpec(a.shape, lambda i, s: (0,) * len(a.shape))
    return pl.pallas_call(
        partial(input_kernel, tile=256),
        out_shape=jax.ShapeDtypeStruct(gz.shape, F32),
        grid_spec=pltpu.PrefetchScalarGridSpec(
            num_scalar_prefetch=1, grid=(1,), in_specs=[whole(a) for a in args], out_specs=whole(gz)),
        compiler_params=pltpu.CompilerParams(vmem_limit_bytes=VMEM_BYTES),
        cost_estimate=pl.CostEstimate(flops=1_600_000_000, bytes_accessed=9_000_000, transcendentals=0),
        name="input_gradient",
    )(scalars, *args)


def send_tensor(a):
    n = lax.axis_size("tensor")
    return lax.ppermute(a, "tensor", [(i, (i + 1) % n) for i in range(n)])


def send_bit(a, bit):
    return lax.ppermute(a, "dp", [(i, i ^ (1 << bit)) for i in range(lax.axis_size("dp"))])


def pick(a, axis, index):
    return lax.dynamic_index_in_dim(a, index, axis, keepdims=False)


def plus(*members):
    return sum(m.astype(F32) for m in members).astype(BF)


def total_chips(buf):
    me = lax.axis_index("dp")
    bits = list(range(1, lax.axis_size("dp").bit_length() - 1))
    split, rest = bits[:3], bits[3:]
    for bit in split:
        side = (me >> bit) & 1
        half = buf.shape[0] // 2
        away = lax.dynamic_slice_in_dim(buf, (1 - side) * half, half, 0)
        kept = lax.dynamic_slice_in_dim(buf, side * half, half, 0)
        buf = plus(kept, send_bit(away, bit))
    for bit in rest:
        buf = plus(buf, send_bit(buf, bit))
    for bit in reversed(split):
        side = (me >> bit) & 1
        got = send_bit(buf, bit)
        buf = jnp.concatenate([jnp.where(side == 0, buf, got), jnp.where(side == 0, got, buf)], axis=0)
    return buf


def local(hidden_in, w_qkv, qv_bias, w_out, out_bias, gain1, shift1, w_up, up_bias, w_down,
          down_bias, gain2, shift2, lengths, head_perm, cotangent):
    rows, width = hidden_in.shape
    core = lax.axis_index("dp") % 2
    length = lengths[lax.axis_index("tensor")]
    pair = w_qkv.shape[2] // 2
    heads = head_perm.shape[0] // 2
    units = up_bias.shape[0] // 2

    def small_of(i):
        return jnp.concatenate([
            pick(qv_bias.reshape(2, 2, pair), 1, i).reshape(-1),
            pick(up_bias.reshape(2, units), 0, i),
            pick(head_perm.reshape(2, heads), 0, i).astype(F32)])

    small_m = send_tensor(small_of(core))
    wq_m = send_tensor(pick(w_qkv.reshape(3, width, 2, pair), 2, core))
    pack_m = send_tensor(jnp.concatenate([
        pick(w_up.reshape(width, 2, units), 1, core),
        pick(w_down.reshape(2, units, width), 0, core),
        pick(w_out.reshape(2, pair, width), 0, core)], axis=0))
    small_p, wq_p, pack_p = (send_bit(a, 0) for a in (small_m, wq_m, pack_m))

    smalls = [small_of(core), small_of(1 - core), small_m, small_p]
    wqs = [w_qkv, w_qkv, wq_m, wq_p]
    where = [core, 1 - core, 0, 0]
    scalars = [jnp.concatenate([jnp.stack([jnp.int32(where[k]), length]), smalls[k][2 * pair + units:].astype(jnp.int32)])
               for k in range(4)]
    kept = []
    for k in range(4):
        kept.append(attend_forward(hidden_in, wqs[k], smalls[k][: 2 * pair].reshape(2, pair, 1), scalars[k]))
    vec = jnp.stack([out_bias, gain1, shift1, down_bias, gain2, shift2])
    base = jnp.stack([core, length])
    ubs = [up_bias.reshape(1, -1), small_m[2 * pair: 2 * pair + units].reshape(1, -1),
           small_p[2 * pair: 2 * pair + units].reshape(1, -1)]
    out, g_z1, g_attn, ffn_m, ffn_p, dub, common = dense(
        base, hidden_in, cotangent, [a[3] for a in kept], vec, w_out, w_up, w_down, ubs, [pack_m, pack_p])

    ffn_got = send_bit(ffn_p, 0)
    ffn_other = plus(ffn_m[1], ffn_got[1])
    ffn_own = plus(ffn_m[0], ffn_got[0], send_tensor(ffn_other))

    wos = [w_out, w_out, pack_m, pack_p]
    blocks = [core, 1 - core, 2 * units // pair, 2 * units // pair]
    back = {}

    def backward(k):
        qkv, e, inv, ctx = kept[k]
        sc = jnp.concatenate([jnp.stack([jnp.int32(blocks[k])]), scalars[k][1:]])
        back[k] = attend_backward(hidden_in, wos[k], qkv, e, inv, ctx, g_attn, sc)

    def tiny(k, shared):
        sums = back[k][2].reshape(-1)
        line = jnp.concatenate([dub[k], sums, jnp.zeros((-sums.size % width,), F32)]).reshape(-1, width)
        return jnp.concatenate([line, shared, jnp.zeros((16 - line.shape[0] - shared.shape[0], width), F32)], axis=0)

    for k in (1, 3, 2, 0):
        backward(k)
    nothing = jnp.zeros_like(common)
    got = {k: send_bit(jnp.concatenate([back[k][1], tiny(k, common if k == 1 else nothing).astype(BF)], axis=0), 0)
           for k in (1, 3)}
    att_other = plus(jnp.concatenate([back[2][1], tiny(2, common).astype(BF)], axis=0), got[3])
    att_other = jnp.concatenate([att_other[: 4 * pair + 2], plus(att_other[4 * pair + 2:], got[1][4 * pair + 2:])], axis=0)
    att_own = plus(jnp.concatenate([back[0][1], tiny(0, common).astype(BF)], axis=0), got[1], send_tensor(att_other))

    x_grad = input_gradient(base, g_z1, w_qkv, wq_m, wq_p, [back[k][0] for k in range(4)])

    merged = jnp.concatenate([ffn_own, att_own], axis=0)
    merged = jnp.pad(merged, ((0, -merged.shape[0] % 128), (0, 0)))
    line = total_chips(merged)
    mate = send_bit(line, 0)
    a = jnp.where(core == 0, line, mate).astype(F32)
    b = jnp.where(core == 0, mate, line).astype(F32)
    at = [0, width, width + units, width + units + 3 * pair, width + units + 4 * pair]
    d_wu = jnp.concatenate([a[:at[1]], b[:at[1]]], axis=1)
    d_wd = jnp.concatenate([a[at[1]: at[2]], b[at[1]: at[2]]], axis=0)
    turn = lambda v: jnp.swapaxes(v[at[2]: at[3]].reshape(3, pair, width), 1, 2)
    d_wq = jnp.concatenate([turn(a), turn(b)], axis=2)
    d_wo = jnp.concatenate([a[at[3]: at[4]], b[at[3]: at[4]]], axis=0)
    d_ub = jnp.concatenate([a[at[4]], b[at[4]]], axis=0)
    d_qvb = jnp.concatenate([v[at[4] + 1, : 2 * pair].reshape(2, pair) for v in (a, b)], axis=1)
    com = a[at[4] + 2: at[4] + 8]
    return (out, x_grad, d_wq, d_qvb, d_wo, com[0], com[1], com[2], d_wu, d_ub, d_wd, com[3], com[4], com[5])


def solution(mesh):
    whole = P()
    rows = P(("dp", "tensor"), None)
    return jax.shard_map(
        local,
        mesh=mesh,
        in_specs=(rows, P(None, None, "tensor"), P(None, "tensor"), P("tensor", None), whole, whole, whole,
                  P(None, "tensor"), P("tensor"), P("tensor", None), whole, whole, whole, P("dp"), P("tensor"), rows),
        out_specs=(rows, rows, P(None, None, "tensor"), P(None, "tensor"), P("tensor", None), whole, whole, whole,
                   P(None, "tensor"), P("tensor"), P("tensor", None), whole, whole, whole),
        check_vma=False,
    )
```

```python
import math
from functools import partial

import jax
import jax.numpy as jnp
from jax import lax
from jax.experimental import pallas as pl
from jax.experimental.pallas import tpu as pltpu
from jax.sharding import PartitionSpec as P

EPSILON = 1e-05
BF = jnp.bfloat16
F32 = jnp.float32
SMALL_ROWS = 64


def dot(a, b, ca, cb):
    return lax.dot_general(a, b, (((ca,), (cb,)), ((), ())), preferred_element_type=F32)


def place(index, size):
    return pl.ds(pl.multiple_of(index * size, size), size)


def whole(a):
    return pl.BlockSpec(a.shape, lambda *_: (0,) * len(a.shape))


def params(mebibytes):
    return pltpu.CompilerParams(vmem_limit_bytes=mebibytes * 1024 * 1024)


def cost(micros, size):
    return pl.CostEstimate(flops=int(micros * 1.1e9), bytes_accessed=size, transcendentals=0)


def forward_kernel(ids, x_ref, w_ref, bias_ref, *rest, slot):
    qkv_ref, e_ref, inv_ref, ctx_ref = rest[-4:]
    width, rows = qkv_ref.shape[1:]
    half = rows // 2
    heads = e_ref.shape[1]
    size = width // heads
    quarter = ids[0] ^ (slot % 2)
    i = pl.program_id(0)

    @pl.when(i == 0)
    def _():
        for c in range(3):
            part = dot(w_ref[c], x_ref[...], 0, 1)
            if c != 1:
                bias = bias_ref[c // 2: c // 2 + 1, place(quarter, width)]
                part = part + jnp.broadcast_to(bias, (width, width)).T[:, :1]
            qkv_ref[c] = part.astype(BF)

    mine = place(i, half)
    factor = math.log2(math.e) / math.sqrt(size)
    for h in range(heads):
        lanes = slice(h * size, (h + 1) * size)
        j = i ^ ids[4 + (slot // 2 * 2 + quarter) * heads + h]
        theirs = place(j, half)
        s = dot(qkv_ref[1, lanes, theirs], qkv_ref[0, lanes, mine], 0, 0)
        key = lax.broadcasted_iota(jnp.int32, (half, 1), 0) + j * half
        s = jnp.where(key < ids[1], s, -1e30)
        top = jnp.max(s, axis=0, keepdims=True)
        e = jnp.exp2((s - top) * factor)
        inv = 1.0 / jnp.sum(e, axis=0, keepdims=True)
        low = e.astype(BF)
        e_ref[0, h] = low
        inv_ref[0, h] = inv
        ctx = dot(qkv_ref[2, lanes, theirs], low, 1, 0) * inv
        ctx_ref[lanes, mine] = ctx.astype(BF)


def attend_forward(ids, x, w, bias, slot, heads, pair, waits=()):
    rows, width = x.shape
    half = rows // 2
    fixed = lambda *shape: pl.BlockSpec(shape, lambda i, *_: (0,) * len(shape))
    return pl.pallas_call(
        partial(forward_kernel, slot=slot),
        out_shape=(
            pltpu.HBM((3, pair, rows), BF),
            pltpu.HBM((2, heads, half, half), BF),
            pltpu.HBM((2, heads, 1, half), F32),
            pltpu.HBM((pair, rows), BF),
        ),
        grid_spec=pltpu.PrefetchScalarGridSpec(
            num_scalar_prefetch=1,
            grid=(2,),
            in_specs=[
                fixed(rows, width),
                pl.BlockSpec((3, width, pair), lambda i, s, *_: (0, 0, (s[0] ^ slot) if slot < 2 else 0)),
                fixed(*bias.shape),
                *[pl.BlockSpec(memory_space=pl.ANY) for _ in waits],
            ],
            out_specs=(
                fixed(3, pair, rows),
                pl.BlockSpec((1, heads, half, half), lambda i, *_: (i, 0, 0, 0)),
                pl.BlockSpec((1, heads, 1, half), lambda i, *_: (i, 0, 0, 0)),
                fixed(pair, rows),
            ),
        ),
        compiler_params=params(16),
        cost_estimate=cost(0.5, 400_000),
        name="attend_forward",
    )(ids, x, w, bias, *waits)


def backward_kernel(ids, x_ref, wo_ref, qkv_ref, e_ref, inv_ref, ctx_ref, ga_ref, small_ref, *rest, slot):
    g_ref, dw_ref, gc_ref = rest[-3:]
    width, rows = gc_ref.shape
    half = rows // 2
    heads = e_ref.shape[1]
    size = width // heads
    quarter = ids[0] ^ (slot % 2)
    i = pl.program_id(0)

    @pl.when(i == 0)
    def _():
        gc_ref[...] = dot(wo_ref[...], ga_ref[...], 1, 1).astype(BF)
        dw_ref[3 * width: 4 * width] = dot(ctx_ref[...], ga_ref[...], 1, 0).astype(BF)

    mine = place(i, half)
    scaling = 1.0 / math.sqrt(size)
    for h in range(heads):
        lanes = slice(h * size, (h + 1) * size)
        j = i ^ ids[4 + (slot // 2 * 2 + quarter) * heads + h]
        theirs = place(j, half)
        g = gc_ref[lanes, mine].astype(F32) * inv_ref[0, h]
        inner = jnp.sum(g * ctx_ref[lanes, mine].astype(F32), axis=0, keepdims=True)
        g = g.astype(BF)
        e = e_ref[0, h]
        dp = dot(qkv_ref[2, lanes, theirs], g, 0, 0)
        ds = (e.astype(F32) * (dp - inner)).astype(BF)
        g_ref[2, lanes, theirs] = dot(g, e, 1, 1).astype(BF)
        g_ref[1, lanes, theirs] = (dot(qkv_ref[0, lanes, mine], ds, 1, 1) * scaling).astype(BF)
        g_ref[0, lanes, mine] = (dot(qkv_ref[1, lanes, theirs], ds, 1, 0) * scaling).astype(BF)

    @pl.when(i == 1)
    def _():
        small = small_ref[0]
        row = lax.broadcasted_iota(jnp.int32, small.shape, 0)
        for c in range(3):
            dw_ref[c * width: (c + 1) * width] = dot(g_ref[c], x_ref[...], 1, 0).astype(BF)
        ones = jnp.ones((8, rows), BF)
        sums = jnp.concatenate([dot(ones, g_ref[c], 1, 1) for c in (0, 2)] * 2, axis=1)
        small = jnp.where(row == 1, sums, small)
        small = jnp.concatenate([small, jnp.zeros((SMALL_ROWS - 8, small.shape[1]), F32)], axis=0)
        dw_ref[4 * width:] = small.astype(BF)


def attend_backward(ids, x, wo, block, kept, g_attn, small, slot, waits=()):
    qkv, e, inv, ctx = kept
    rows, width = x.shape
    heads = e.shape[1]
    pair = ctx.shape[0]
    half = rows // 2
    fixed = lambda *shape: pl.BlockSpec(shape, lambda i, *_: (0,) * len(shape))
    return pl.pallas_call(
        partial(backward_kernel, slot=slot),
        out_shape=(
            jax.ShapeDtypeStruct((3, pair, rows), BF),
            jax.ShapeDtypeStruct((4 * pair + SMALL_ROWS, width), BF),
        ),
        grid_spec=pltpu.PrefetchScalarGridSpec(
            num_scalar_prefetch=1,
            grid=(2,),
            in_specs=[
                fixed(rows, width),
                pl.BlockSpec((pair, width), lambda i, s: (block(s[0]), 0)),
                fixed(3, pair, rows),
                pl.BlockSpec((1, heads, half, half), lambda i, *_: (i, 0, 0, 0)),
                pl.BlockSpec((1, heads, 1, half), lambda i, *_: (i, 0, 0, 0)),
                fixed(pair, rows),
                fixed(rows, width),
                pl.BlockSpec((1, 8, width), lambda i, *_: (slot, 0, 0)),
                *[pl.BlockSpec(memory_space=pl.ANY) for _ in waits],
            ],
            out_specs=(fixed(3, pair, rows), fixed(4 * pair + SMALL_ROWS, width)),
            scratch_shapes=[pltpu.VMEM((pair, rows), BF)],
        ),
        compiler_params=params(16),
        cost_estimate=cost(7.8, 4_000_000),
        name="attend_backward",
    )(ids, x, wo, qkv, e, inv, ctx, g_attn, small, *waits)


def normed(v):
    centre = v - jnp.mean(v, axis=-1, keepdims=True)
    inv = lax.rsqrt(jnp.mean(centre * centre, axis=-1, keepdims=True) + EPSILON)
    return centre * inv, inv


def norm_back(g, hat, inv, gain):
    g = g * gain
    return (g - jnp.mean(g, axis=-1, keepdims=True) - hat * jnp.mean(g * hat, axis=-1, keepdims=True)) * inv


def gelu_parts(v):
    t = 1.0 / (1.0 + (0.3275911 * math.sqrt(0.5)) * jnp.abs(v))
    bell = jnp.exp2(v * v * (-0.5 * math.log2(math.e)))
    poly = ((((0.5 * 1.061405429 * t - 0.5 * 1.453152027) * t + 0.5 * 1.421413741) * t
             - 0.5 * 0.284496736) * t + 0.5 * 0.254829592) * t
    tail = poly * bell
    cdf = jnp.where(v < 0, tail, 1.0 - tail)
    return v * cdf, cdf + v * bell * (1.0 / math.sqrt(2.0 * math.pi))


def dense_kernel(ids, x_ref, cot_ref, c0, c1, c2, c3, out_bias, gain1, shift1, down_bias, gain2, shift2,
                 wo_own, wu_own, wd_own, ub_own, wo_m, wu_m, wd_m, ub_other, wo_p, wu_p, wd_p,
                 out_ref, gz_ref, ga_ref, gm_ref, gp_ref, small_ref,
                 wo_all, n1_all, gf_all, act_all, gp_all, tile):
    rows, width = x_ref.shape
    pair = c0.shape[0]
    units = ub_own.shape[1] // 2
    core, length = ids[0], ids[1]

    wo_all[0:pair] = wo_own[place(core, pair)]
    wo_all[pair: 2 * pair] = wo_own[place(1 - core, pair)]
    wo_all[2 * pair: 3 * pair] = wo_m[...]
    wo_all[3 * pair:] = wo_p[...]
    near, far = place(core, units), place(1 - core, units)
    ups = [wu_own.at[:, near], wu_own.at[:, far], wu_m, wu_p]
    downs = [wd_own.at[near], wd_own.at[far], wd_m, wd_p]
    biases = [ub_own.at[:, near], ub_own.at[:, far],
              ub_other.at[:, near], ub_other.at[:, far]]
    small_ref[...] = jnp.zeros_like(small_ref)

    @pl.loop(0, rows // tile)
    def _(r):
        here = place(r, tile)
        ctx = jnp.concatenate([c[:, here] for c in (c0, c1, c2, c3)], axis=0)
        z1 = x_ref[here].astype(F32) + dot(ctx, wo_all[...], 0, 0) + out_bias[...]
        hat1, inv1 = normed(z1)
        n1 = hat1 * gain1[...] + shift1[...]
        low = n1.astype(BF)
        n1_all[here] = low
        z2 = n1 + down_bias[...]
        for k in range(4):
            cols = slice(k * units, (k + 1) * units)
            act, slope = gelu_parts(dot(low, ups[k][...], 1, 0) + biases[k][...])
            act = act.astype(BF)
            act_all[here, cols] = act
            gp_all[here, cols] = slope.astype(BF)
            z2 = z2 + dot(act, downs[k][...], 1, 0)
        hat2, inv2 = normed(z2)
        row = lax.broadcasted_iota(jnp.int32, (tile, 1), 0) + r * tile
        valid = (row < length).astype(F32)
        out_ref[here] = ((hat2 * gain2[...] + shift2[...]) * valid).astype(BF)
        g_out = cot_ref[here].astype(F32) * valid
        g_z2 = norm_back(g_out, hat2, inv2, gain2[...])
        g_ffn = g_z2.astype(BF)
        gf_all[here] = g_ffn
        g_n1 = g_z2
        for k in range(4):
            cols = slice(k * units, (k + 1) * units)
            g_pre = (dot(g_ffn, downs[k][...], 1, 1) * gp_all[here, cols].astype(F32)).astype(BF)
            gp_all[here, cols] = g_pre
            small_ref[k, 0:1] += jnp.sum(g_pre.astype(F32), axis=0, keepdims=True)
            g_n1 = g_n1 + dot(g_pre, ups[k][...], 1, 1)
        g_z1 = norm_back(g_n1, hat1, inv1, gain1[...])
        gz_ref[here] = g_z1
        g_attn = g_z1.astype(BF)
        ga_ref[here] = g_attn
        sums = (g_attn.astype(F32), g_n1 * hat1, g_n1, g_ffn.astype(F32), g_out * hat2, g_out)
        for k, v in enumerate(sums):
            small_ref[0, 2 + k: 3 + k] += jnp.sum(v, axis=0, keepdims=True)

    for k in range(1, 4):
        small_ref[k, 2:8] = small_ref[0, 2:8]
    flipped = n1_all[...].T
    for k in range(4):
        cols = slice(k * units, (k + 1) * units)
        to = (gm_ref, gp_ref)[k % 2].at[k // 2]
        to[:width] = dot(flipped, gp_all[:, cols], 1, 0).astype(BF)
        to[width:] = dot(act_all[:, cols], gf_all[...], 0, 0).astype(BF)


def dense(ids, x, cot, ctxs, vecs, own, other):
    rows, width = x.shape
    pair = ctxs[0].shape[0]
    units = own[3].shape[1] // 2
    args = [x, cot, *ctxs, *vecs, *own, *other]
    outs = (
        jax.ShapeDtypeStruct((rows, width), BF),
        jax.ShapeDtypeStruct((rows, width), F32),
        jax.ShapeDtypeStruct((rows, width), BF),
        jax.ShapeDtypeStruct((2, width + units, width), BF),
        jax.ShapeDtypeStruct((2, width + units, width), BF),
        jax.ShapeDtypeStruct((4, 8, width), F32),
    )
    return pl.pallas_call(
        partial(dense_kernel, tile=256),
        out_shape=outs,
        grid_spec=pltpu.PrefetchScalarGridSpec(
            num_scalar_prefetch=1,
            grid=(1,),
            in_specs=[whole(a) for a in args],
            out_specs=tuple(whole(a) for a in outs),
            scratch_shapes=[
                pltpu.VMEM((4 * pair, width), BF),
                pltpu.VMEM((rows, width), BF),
                pltpu.VMEM((rows, width), BF),
                pltpu.VMEM((rows, 4 * units), BF),
                pltpu.VMEM((rows, 4 * units), BF),
            ],
        ),
        compiler_params=params(36),
        cost_estimate=cost(31, 20_000_000),
        name="dense",
    )(ids, *args)


def input_kernel(ids, gz_ref, w_own, w_m, w_p, g0, g1, g2, g3, *rest, tile):
    out_ref = rest[-1]
    rows, width = gz_ref.shape
    pair = g0.shape[1]
    core = ids[0]

    @pl.loop(0, rows // tile)
    def _(r):
        here = place(r, tile)
        total = gz_ref[here]
        for c in range(3):
            g = jnp.concatenate([g0[c, :, here], g1[c, :, here], g2[c, :, here], g3[c, :, here]], axis=0)
            w = jnp.concatenate([w_own[c, :, place(core, pair)], w_own[c, :, place(1 - core, pair)], w_m[c], w_p[c]], axis=1)
            total = total + dot(g, w, 0, 1)
        out_ref[here] = total


def input_gradient(ids, gz, w_own, w_m, w_p, gs, waits=()):
    args = [gz, w_own, w_m, w_p, *gs]
    return pl.pallas_call(
        partial(input_kernel, tile=256),
        out_shape=jax.ShapeDtypeStruct(gz.shape, F32),
        grid_spec=pltpu.PrefetchScalarGridSpec(
            num_scalar_prefetch=1, grid=(1,),
            in_specs=[whole(a) for a in args] + [pl.BlockSpec(memory_space=pl.ANY) for _ in waits],
            out_specs=whole(gz)),
        compiler_params=params(20),
        cost_estimate=cost(7, 9_000_000),
        name="input_gradient",
    )(ids, *args, *waits)


def attention_kernel(ids, mine_near, mine_far, mate_near, mate_far, dwq_ref, dqb_ref, dwo_ref, dub_ref,
                     v0, v1, v2, v3, v4, v5, both):
    core, side = ids[0], ids[2]
    part = mine_near.shape[0]
    pair = dwo_ref.shape[0] // 2
    units = dub_ref.shape[1] // 2
    for c, near, far in ((core, mine_near, mine_far), (1 - core, mate_near, mate_far)):
        both[c, pl.ds(pl.multiple_of(side * part, 8), part)] = near[...].astype(F32)
        both[c, pl.ds(pl.multiple_of((1 - side) * part, 8), part)] = far[...].astype(F32)
    for m in range(2):
        cols = slice(m * pair, (m + 1) * pair)
        for c in range(3):
            dwq_ref[c, :, cols] = both[m, c * pair: (c + 1) * pair].T
        dwo_ref[cols] = both[m, 3 * pair: 4 * pair]
        dub_ref[:, m * units: (m + 1) * units] = both[m, 4 * pair: 4 * pair + 1]
        for c in range(2):
            dqb_ref[c: c + 1, cols] = both[m, 4 * pair + 1: 4 * pair + 2, c * pair: (c + 1) * pair]
    for k, ref in enumerate((v0, v1, v2, v3, v4, v5)):
        ref[...] = both[0, 4 * pair + 2 + k: 4 * pair + 3 + k]


def assemble_attention(ids, parts, pair, units):
    width = parts[0].shape[1]
    outs = [(3, width, 2 * pair), (2, 2 * pair), (2 * pair, width), (1, 2 * units)] + [(1, width)] * 6
    outs = tuple(jax.ShapeDtypeStruct(s, F32) for s in outs)
    return pl.pallas_call(
        attention_kernel,
        out_shape=outs,
        grid_spec=pltpu.PrefetchScalarGridSpec(
            num_scalar_prefetch=1, grid=(1,), in_specs=[whole(a) for a in parts],
            out_specs=tuple(whole(a) for a in outs),
            scratch_shapes=[pltpu.VMEM((2, 2 * parts[0].shape[0], width), F32)]),
        compiler_params=params(16),
        cost_estimate=cost(3, 4_000_000),
        name="assemble_attention",
    )(ids, *parts)


def dense_out_kernel(ids, mine_near, mine_far, mate_near, mate_far, dwu_ref, dwd_ref):
    core, side = ids[0], ids[2]
    units = mine_near.shape[1]
    part = mine_near.shape[0] // 2
    width = dwu_ref.shape[0]
    for c, near, far in ((core, mine_near, mine_far), (1 - core, mate_near, mate_far)):
        for s, ref in ((side, near), (1 - side, far)):
            dwu_ref[place(s, part), place(c, units)] = ref[:part].astype(F32)
            dwd_ref[pl.ds(pl.multiple_of(c * width + s * part, part), part)] = ref[part:].astype(F32)


def assemble_dense(ids, parts, units):
    width = parts[0].shape[1]
    outs = tuple(jax.ShapeDtypeStruct(s, F32) for s in ((width, 2 * units), (2 * units, width)))
    return pl.pallas_call(
        dense_out_kernel,
        out_shape=outs,
        grid_spec=pltpu.PrefetchScalarGridSpec(
            num_scalar_prefetch=1, grid=(1,), in_specs=[whole(a) for a in parts],
            out_specs=tuple(whole(a) for a in outs)),
        compiler_params=params(20),
        cost_estimate=cost(3, 6_000_000),
        name="assemble_dense",
    )(ids, *parts)


def send_tensor(a):
    n = lax.axis_size("tensor")
    return lax.ppermute(a, "tensor", [(i, (i + 1) % n) for i in range(n)])


def send_bit(a, bit):
    return lax.ppermute(a, "dp", [(i, i ^ (1 << bit)) for i in range(lax.axis_size("dp"))])


def plus(*members):
    return sum(m.astype(F32) for m in members).astype(BF)


def tie(*arrays):
    return lax.optimization_barrier(arrays)


def half_of(a, side, axis=0):
    n = a.shape[axis] // 2
    return lax.dynamic_slice_in_dim(a, side * n, n, axis)


def joined(mine, got, side, axis=0):
    return jnp.concatenate([jnp.where(side == 0, mine, got), jnp.where(side == 0, got, mine)], axis=axis)


def local(hidden_in, w_qkv, qv_bias, w_out, out_bias, gain1, shift1, w_up, up_bias, w_down,
          down_bias, gain2, shift2, lengths, head_perm, cotangent):
    rows, width = hidden_in.shape
    me = lax.axis_index("dp")
    core, xside, zside = me & 1, (me >> 1) & 1, (me >> 2) & 1
    upper_bits = range(3, lax.axis_size("dp").bit_length() - 1)
    pair = w_qkv.shape[2] // 2
    heads = head_perm.shape[0] // 2
    units = up_bias.shape[0] // 2
    row = lambda v: v.reshape(1, -1)
    def fetch(a, axis, rows_axis):
        sizes = list(a.shape)
        starts = [0] * a.ndim
        for dim, index in ((axis, core), (rows_axis, xside)):
            sizes[dim] //= 2
            starts[dim] += index * sizes[dim]
        return lax.dynamic_slice(a, starts, sizes)

    def forward(slot, w, bias, waits=()):
        return attend_forward(ids, hidden_in, w, bias, slot, heads, pair, waits)

    perm_other, bias_other, ub_other = send_tensor(head_perm), send_tensor(qv_bias), send_tensor(up_bias)
    pieces = [fetch(w_qkv, 2, 1), fetch(w_up, 1, 0), fetch(w_down, 0, 0), fetch(w_out, 0, 0)]
    *pieces, perm_other, bias_other, ub_other = tie(*pieces, perm_other, bias_other, ub_other)
    wq_m, wu_m, wd_m, wo_m = (send_tensor(a) for a in pieces)
    ids = jnp.concatenate([core.reshape(1), lax.dynamic_slice_in_dim(lengths, lax.axis_index("tensor"), 1, 0),
                             xside.reshape(1), zside.reshape(1), head_perm, perm_other])
    kept = [forward(0, w_qkv, qv_bias, pieces)]
    wq_m, ctx = tie(wq_m, kept[0][3])
    wq_got = send_bit(wq_m, 1)
    kept.append(forward(1, w_qkv, qv_bias))
    wq_got, wu_m, ctx1 = tie(wq_got, wu_m, kept[1][3])
    wu_got = send_bit(wu_m, 1)
    wq_m = joined(wq_m, wq_got, xside, 1)
    wq_p = send_bit(wq_m, 0)
    kept.append(forward(2, wq_m, bias_other))
    wd_m, wo_m, wu_got, ctx2 = tie(wd_m, wo_m, wu_got, kept[2][3])
    wd_got, wo_got = send_bit(wd_m, 1), send_bit(wo_m, 1)
    wu_m = joined(wu_m, wu_got, xside)
    wu_p = send_bit(wu_m, 0)
    kept.append(forward(3, wq_p, bias_other))
    wd_got, wo_got, wu_p, ctx3 = tie(wd_got, wo_got, wu_p, kept[3][3])
    wd_m, wo_m = joined(wd_m, wd_got, xside), joined(wo_m, wo_got, xside)
    ctxs = [ctx, ctx1, ctx2, ctx3]
    wo_p, wd_p = send_bit(wo_m, 0), send_bit(wd_m, 0)
    out, g_z1, g_attn, ffn_m, ffn_p, smalls = dense(
        ids, hidden_in, cotangent, ctxs,
        [row(v) for v in (out_bias, gain1, shift1, down_bias, gain2, shift2)],
        [w_out, w_up, w_down, row(up_bias)], [wo_m, wu_m, wd_m, row(ub_other), wo_p, wu_p, wd_p])

    def backward(k, waits=()):
        if k < 2:
            wo, block = w_out, lambda c: c ^ k
        else:
            wo, block = (wo_m, wo_p)[k - 2], lambda c: 0
        return attend_backward(ids, hidden_in, wo, block, kept[k], g_attn, smalls, k, waits)

    ffn_got = send_bit(ffn_p, 0)
    up = [(ffn_m[t, :width], ffn_got[t, :width]) for t in range(2)]
    down = [(ffn_m[t, width:], ffn_got[t, width:]) for t in range(2)]
    up_other = plus(*up[1])
    up_got = send_tensor(up_other)
    down_away = jnp.stack([plus(*[half_of(v, 1 - xside) for v in down[t]]) for t in range(2)])
    down_got = send_bit(down_away, 1)
    g3, d3 = backward(3, (up_other, down_away))
    d3_got = send_bit(d3, 0)
    g2, d2 = backward(2, (d3,))
    other_away = plus(*[half_of(v, 1 - xside) for v in (d2, d3_got)])
    other_got = send_bit(other_away, 1)
    g1, d1 = backward(1, (other_away,))
    d1, up_got, down_got = tie(d1, up_got, down_got)
    d1_got = send_bit(d1, 0)
    up_away = plus(*[half_of(v, 1 - xside) for v in (*up[0], up_got)])
    down_other = plus(*[half_of(v, xside) for v in down[1]], down_got[1])
    up_away, down_other, other_got = tie(up_away, down_other, other_got)
    att_other = plus(*[half_of(v, xside) for v in (d2, d3_got)], other_got)
    up_got2 = send_bit(up_away, 1)
    down_got2 = send_tensor(down_other)
    att_got = send_tensor(att_other)
    g0, d0 = backward(0, (up_away, down_other, att_other))
    att_away = plus(*[half_of(v, 1 - xside) for v in (d0, d1_got)])
    att_got2 = send_bit(att_away, 1)
    att_away, up_got2, down_got2 = tie(att_away, up_got2, down_got2)
    ffn = jnp.concatenate([
        plus(*[half_of(v, xside) for v in (*up[0], up_got)], up_got2),
        plus(*[half_of(v, xside) for v in down[0]], down_got[0], down_got2)], axis=0)
    ffn_away = half_of(ffn, 1 - zside)
    ffn_got2 = send_bit(ffn_away, 2)
    x_grad = input_gradient(ids, g_z1, w_qkv, wq_m, wq_p, [g0, g1, g2, g3], (att_away, ffn_away))
    x_grad, att_got, att_got2, ffn_got2 = tie(x_grad, att_got, att_got2, ffn_got2)
    att = plus(*[half_of(v, xside) for v in (d0, d1_got)], att_got, att_got2)
    att_got3 = send_bit(half_of(att, 1 - zside), 2)
    ffn = plus(half_of(ffn, zside), ffn_got2)
    att = plus(half_of(att, zside), att_got3)
    for bit in upper_bits:
        ffn, att = plus(ffn, send_bit(ffn, bit)), plus(att, send_bit(att, bit))
    ffn = joined(ffn, send_bit(ffn, 2), zside)
    att = joined(att, send_bit(att, 2), zside)
    ffn_far = send_bit(ffn, 1)
    att_far = send_bit(att, 1)
    d_wu, d_wd = assemble_dense(ids, [ffn, ffn_far, send_bit(ffn, 0), send_bit(ffn_far, 0)], units)
    d_wu, att_far = tie(d_wu, att_far)
    d_wq, d_qb, d_wo, d_ub, *vecs = assemble_attention(
        ids, [att, att_far, send_bit(att, 0), send_bit(att_far, 0)], pair, units)
    v = [a.reshape(-1) for a in vecs]
    return (out, x_grad, d_wq, d_qb, d_wo, v[0], v[1], v[2], d_wu, d_ub.reshape(-1), d_wd, v[3], v[4], v[5])


def solution(mesh):
    every = P()
    rows = P(("dp", "tensor"), None)
    return jax.shard_map(
        local,
        mesh=mesh,
        in_specs=(rows, P(None, None, "tensor"), P(None, "tensor"), P("tensor", None), every, every, every,
                  P(None, "tensor"), P("tensor"), P("tensor", None), every, every, every, P("dp"), P("tensor"), rows),
        out_specs=(rows, rows, P(None, None, "tensor"), P(None, "tensor"), P("tensor", None), every, every, every,
                   P(None, "tensor"), P("tensor"), P("tensor", None), every, every, every),
        check_vma=False,
    )
```

```python
import math
from functools import partial

import jax
import jax.numpy as jnp
from jax import lax
from jax.experimental import pallas as pl
from jax.experimental.pallas import tpu as pltpu
from jax.sharding import PartitionSpec as P

EPSILON = 1e-05
BF = jnp.bfloat16
F32 = jnp.float32
SMALL_ROWS = 64


def dot(a, b, ca, cb):
    return lax.dot_general(a, b, (((ca,), (cb,)), ((), ())), preferred_element_type=F32)


def place(index, size):
    return pl.ds(pl.multiple_of(index * size, size), size)


def whole(a):
    return pl.BlockSpec(a.shape, lambda *_: (0,) * len(a.shape))


def params(mebibytes):
    return pltpu.CompilerParams(vmem_limit_bytes=mebibytes * 1024 * 1024)


def cost(micros, size):
    return pl.CostEstimate(flops=int(micros * 1.1e9), bytes_accessed=size, transcendentals=0)


def forward_kernel(ids, lengths, perm, x_ref, w_ref, bias_ref, *rest, slot):
    qkv_ref, e_ref, inv_ref, ctx_ref = rest[-4:]
    width, rows = qkv_ref.shape[1:]
    half = rows // 2
    heads = e_ref.shape[1]
    size = width // heads
    quarter = ids[0] ^ (slot % 2)
    i = pl.program_id(0)

    @pl.when(i == 0)
    def _():
        every = dot(jnp.concatenate([w_ref[c] for c in range(3)], axis=1), x_ref[...], 0, 1)
        for c in range(3):
            part = every[c * width: (c + 1) * width]
            if c != 1:
                bias = bias_ref[c // 2: c // 2 + 1, place(quarter, width)]
                part = part + jnp.broadcast_to(bias, (width, width)).T[:, :1]
            qkv_ref[c] = part.astype(BF)

    mine = place(i, half)
    factor = math.log2(math.e) / math.sqrt(size)
    scores = []
    for h in range(heads):
        lanes = slice(h * size, (h + 1) * size)
        theirs = place(i ^ perm[quarter * heads + h], half)
        scores.append(dot(qkv_ref[1, lanes, theirs], qkv_ref[0, lanes, mine], 0, 0))
    for h in range(heads):
        lanes = slice(h * size, (h + 1) * size)
        j = i ^ perm[quarter * heads + h]
        theirs = place(j, half)
        s = scores[h]
        key = lax.broadcasted_iota(jnp.int32, (half, 1), 0) + j * half
        s = jnp.where(key < lengths[ids[1]], s, -1e30)
        top = jnp.max(s, axis=0, keepdims=True)
        e = jnp.exp2((s - top) * factor)
        inv = 1.0 / jnp.sum(e, axis=0, keepdims=True)
        low = e.astype(BF)
        e_ref[0, h] = low
        inv_ref[0, h] = inv
        ctx = dot(qkv_ref[2, lanes, theirs], low, 1, 0) * inv
        ctx_ref[lanes, mine] = ctx.astype(BF)


def attend_forward(ids, lengths, perm, x, w, bias, slot, heads, pair, waits=()):
    rows, width = x.shape
    half = rows // 2
    fixed = lambda *shape: pl.BlockSpec(shape, lambda i, *_: (0,) * len(shape))
    return pl.pallas_call(
        partial(forward_kernel, slot=slot),
        out_shape=(
            pltpu.HBM((3, pair, rows), BF),
            pltpu.HBM((2, heads, half, half), BF),
            pltpu.HBM((2, heads, 1, half), F32),
            pltpu.HBM((pair, rows), BF),
        ),
        grid_spec=pltpu.PrefetchScalarGridSpec(
            num_scalar_prefetch=3,
            grid=(2,),
            in_specs=[
                fixed(rows, width),
                pl.BlockSpec((3, width, pair), lambda i, s, *_: (0, 0, (s[0] ^ slot) if slot < 2 else 0)),
                fixed(*bias.shape),
                *[pl.BlockSpec(memory_space=pl.ANY) for _ in waits],
            ],
            out_specs=(
                fixed(3, pair, rows),
                pl.BlockSpec((1, heads, half, half), lambda i, *_: (i, 0, 0, 0)),
                pl.BlockSpec((1, heads, 1, half), lambda i, *_: (i, 0, 0, 0)),
                fixed(pair, rows),
            ),
        ),
        compiler_params=params(16),
        cost_estimate=cost(0.5, 400_000),
        name="attend_forward",
    )(ids, lengths, perm, x, w, bias, *waits)


def backward_kernel(ids, perm, x_ref, wo_ref, qkv_ref, e_ref, inv_ref, ctx_ref, ga_ref, small_ref, *rest, slot):
    g_ref, dw_ref, gc_ref = rest[-3:]
    width, rows = gc_ref.shape
    half = rows // 2
    heads = e_ref.shape[1]
    size = width // heads
    quarter = ids[0] ^ (slot % 2)
    i = pl.program_id(0)

    @pl.when(i == 0)
    def _():
        gc_ref[...] = dot(wo_ref[...], ga_ref[...], 1, 1).astype(BF)
        dw_ref[3 * width: 4 * width] = dot(ctx_ref[...], ga_ref[...], 1, 0).astype(BF)

    mine = place(i, half)
    scaling = 1.0 / math.sqrt(size)
    for h in range(heads):
        lanes = slice(h * size, (h + 1) * size)
        j = i ^ perm[quarter * heads + h]
        theirs = place(j, half)
        g = gc_ref[lanes, mine].astype(F32) * inv_ref[0, h]
        inner = jnp.sum(g * ctx_ref[lanes, mine].astype(F32), axis=0, keepdims=True)
        g = g.astype(BF)
        e = e_ref[0, h]
        dp = dot(qkv_ref[2, lanes, theirs], g, 0, 0)
        ds = (e.astype(F32) * (dp - inner)).astype(BF)
        g_ref[2, lanes, theirs] = dot(g, e, 1, 1).astype(BF)
        g_ref[1, lanes, theirs] = (dot(qkv_ref[0, lanes, mine], ds, 1, 1) * scaling).astype(BF)
        g_ref[0, lanes, mine] = (dot(qkv_ref[1, lanes, theirs], ds, 1, 0) * scaling).astype(BF)

    @pl.when(i == 1)
    def _():
        small = small_ref[0]
        row = lax.broadcasted_iota(jnp.int32, small.shape, 0)
        dw_ref[:3 * width] = dot(g_ref[...].reshape(3 * width, rows), x_ref[...], 1, 0).astype(BF)
        ones = jnp.ones((8, rows), BF)
        sums = jnp.concatenate([dot(ones, g_ref[c], 1, 1) for c in (0, 2)] * 2, axis=1)
        small = jnp.where(row == 1, sums, small)
        small = jnp.concatenate([small, jnp.zeros((SMALL_ROWS - 8, small.shape[1]), F32)], axis=0)
        dw_ref[4 * width:] = small.astype(BF)


def attend_backward(ids, perm, x, wo, block, kept, g_attn, small, slot, waits=()):
    qkv, e, inv, ctx = kept
    rows, width = x.shape
    heads = e.shape[1]
    pair = ctx.shape[0]
    half = rows // 2
    fixed = lambda *shape: pl.BlockSpec(shape, lambda i, *_: (0,) * len(shape))
    return pl.pallas_call(
        partial(backward_kernel, slot=slot),
        out_shape=(
            jax.ShapeDtypeStruct((3, pair, rows), BF),
            jax.ShapeDtypeStruct((4 * pair + SMALL_ROWS, width), BF),
        ),
        grid_spec=pltpu.PrefetchScalarGridSpec(
            num_scalar_prefetch=2,
            grid=(2,),
            in_specs=[
                fixed(rows, width),
                pl.BlockSpec((pair, width), lambda i, s, p: (block(s[0]), 0)),
                fixed(3, pair, rows),
                pl.BlockSpec((1, heads, half, half), lambda i, *_: (i, 0, 0, 0)),
                pl.BlockSpec((1, heads, 1, half), lambda i, *_: (i, 0, 0, 0)),
                fixed(pair, rows),
                fixed(rows, width),
                pl.BlockSpec((1, 8, width), lambda i, *_: (slot, 0, 0)),
                *[pl.BlockSpec(memory_space=pl.ANY) for _ in waits],
            ],
            out_specs=(fixed(3, pair, rows), fixed(4 * pair + SMALL_ROWS, width)),
            scratch_shapes=[pltpu.VMEM((pair, rows), BF)],
        ),
        compiler_params=params(16),
        cost_estimate=cost(7.8, 4_000_000),
        name="attend_backward",
    )(ids, perm, x, wo, qkv, e, inv, ctx, g_attn, small, *waits)


def normed(v):
    centre = v - jnp.mean(v, axis=-1, keepdims=True)
    inv = lax.rsqrt(jnp.mean(centre * centre, axis=-1, keepdims=True) + EPSILON)
    return centre * inv, inv


def norm_back(g, hat, inv, gain):
    g = g * gain
    return (g - jnp.mean(g, axis=-1, keepdims=True) - hat * jnp.mean(g * hat, axis=-1, keepdims=True)) * inv


def gelu_parts(v):
    t = 1.0 / (1.0 + (0.3275911 * math.sqrt(0.5)) * jnp.abs(v))
    bell = jnp.exp2(v * v * (-0.5 * math.log2(math.e)))
    poly = ((((0.5 * 1.061405429 * t - 0.5 * 1.453152027) * t + 0.5 * 1.421413741) * t
             - 0.5 * 0.284496736) * t + 0.5 * 0.254829592) * t
    tail = poly * bell
    cdf = jnp.where(v < 0, tail, 1.0 - tail)
    return v * cdf, cdf + v * bell * (1.0 / math.sqrt(2.0 * math.pi))


def dense_kernel(ids, lengths, x_ref, cot_ref, c0, c1, c2, c3, out_bias, gain1, shift1, down_bias, gain2, shift2,
                 wo_own, wu_own, wd_own, ub_own, wo_m, wu_m, wd_m, ub_other, wo_p, wu_p, wd_p,
                 out_ref, gz_ref, ga_ref, gm_ref, gp_ref, small_ref,
                 wo_all, n1_all, gf_all, act_all, gp_all, tile):
    rows, width = x_ref.shape
    pair = c0.shape[0]
    units = ub_own.shape[1] // 2
    core, length = ids[0], lengths[ids[1]]

    wo_all[0:pair] = wo_own[place(core, pair)]
    wo_all[pair: 2 * pair] = wo_own[place(1 - core, pair)]
    wo_all[2 * pair: 3 * pair] = wo_m[...]
    wo_all[3 * pair:] = wo_p[...]
    near, far = place(core, units), place(1 - core, units)
    ups = [wu_own.at[:, near], wu_own.at[:, far], wu_m, wu_p]
    downs = [wd_own.at[near], wd_own.at[far], wd_m, wd_p]
    biases = [ub_own.at[:, near], ub_own.at[:, far],
              ub_other.at[:, near], ub_other.at[:, far]]
    small_ref[...] = jnp.zeros_like(small_ref)

    @pl.loop(0, rows // tile, unroll=True)
    def _(r):
        here = place(r, tile)
        ctx = jnp.concatenate([c[:, here] for c in (c0, c1, c2, c3)], axis=0)
        z1 = x_ref[here].astype(F32) + dot(ctx, wo_all[...], 0, 0) + out_bias[...]
        hat1, inv1 = normed(z1)
        n1 = hat1 * gain1[...] + shift1[...]
        low = n1.astype(BF)
        n1_all[here] = low
        z2 = n1 + down_bias[...]
        for k in range(4):
            cols = slice(k * units, (k + 1) * units)
            act, slope = gelu_parts(dot(low, ups[k][...], 1, 0) + biases[k][...])
            act = act.astype(BF)
            act_all[here, cols] = act
            gp_all[here, cols] = slope.astype(BF)
            z2 = z2 + dot(act, downs[k][...], 1, 0)
        hat2, inv2 = normed(z2)
        row = lax.broadcasted_iota(jnp.int32, (tile, 1), 0) + r * tile
        valid = (row < length).astype(F32)
        out_ref[here] = ((hat2 * gain2[...] + shift2[...]) * valid).astype(BF)
        g_out = cot_ref[here].astype(F32) * valid
        g_z2 = norm_back(g_out, hat2, inv2, gain2[...])
        g_ffn = g_z2.astype(BF)
        gf_all[here] = g_ffn
        g_n1 = g_z2
        for k in range(4):
            cols = slice(k * units, (k + 1) * units)
            g_pre = (dot(g_ffn, downs[k][...], 1, 1) * gp_all[here, cols].astype(F32)).astype(BF)
            gp_all[here, cols] = g_pre
            small_ref[k, 0:1] += jnp.sum(g_pre.astype(F32), axis=0, keepdims=True)
            g_n1 = g_n1 + dot(g_pre, ups[k][...], 1, 1)
        g_z1 = norm_back(g_n1, hat1, inv1, gain1[...])
        gz_ref[here] = g_z1
        g_attn = g_z1.astype(BF)
        ga_ref[here] = g_attn
        sums = (g_attn.astype(F32), g_n1 * hat1, g_n1, g_ffn.astype(F32), g_out * hat2, g_out)
        for k, v in enumerate(sums):
            small_ref[0, 2 + k: 3 + k] += jnp.sum(v, axis=0, keepdims=True)

    for k in range(1, 4):
        small_ref[k, 2:8] = small_ref[0, 2:8]
    flipped = n1_all[...].T
    for k in range(4):
        cols = slice(k * units, (k + 1) * units)
        to = (gm_ref, gp_ref)[k % 2].at[k // 2]
        to[:width] = dot(flipped, gp_all[:, cols], 1, 0).astype(BF)
        to[width:] = dot(act_all[:, cols], gf_all[...], 0, 0).astype(BF)


def dense(ids, lengths, x, cot, ctxs, vecs, own, other):
    rows, width = x.shape
    pair = ctxs[0].shape[0]
    units = own[3].shape[1] // 2
    args = [x, cot, *ctxs, *vecs, *own, *other]
    outs = (
        jax.ShapeDtypeStruct((rows, width), BF),
        jax.ShapeDtypeStruct((rows, width), F32),
        jax.ShapeDtypeStruct((rows, width), BF),
        jax.ShapeDtypeStruct((2, width + units, width), BF),
        jax.ShapeDtypeStruct((2, width + units, width), BF),
        jax.ShapeDtypeStruct((4, 8, width), F32),
    )
    return pl.pallas_call(
        partial(dense_kernel, tile=512),
        out_shape=outs,
        grid_spec=pltpu.PrefetchScalarGridSpec(
            num_scalar_prefetch=2,
            grid=(1,),
            in_specs=[whole(a) for a in args],
            out_specs=tuple(whole(a) for a in outs),
            scratch_shapes=[
                pltpu.VMEM((4 * pair, width), BF),
                pltpu.VMEM((rows, width), BF),
                pltpu.VMEM((rows, width), BF),
                pltpu.VMEM((rows, 4 * units), BF),
                pltpu.VMEM((rows, 4 * units), BF),
            ],
        ),
        compiler_params=params(36),
        cost_estimate=cost(31, 20_000_000),
        name="dense",
    )(ids, lengths, *args)


def input_kernel(ids, gz_ref, w_own, w_m, w_p, g0, g1, g2, g3, *rest, tile):
    out_ref = rest[-1]
    rows, width = gz_ref.shape
    pair = g0.shape[1]
    core = ids[0]

    @pl.loop(0, rows // tile)
    def _(r):
        here = place(r, tile)
        total = gz_ref[here]
        for c in range(3):
            g = jnp.concatenate([g0[c, :, here], g1[c, :, here], g2[c, :, here], g3[c, :, here]], axis=0)
            w = jnp.concatenate([w_own[c, :, place(core, pair)], w_own[c, :, place(1 - core, pair)], w_m[c], w_p[c]], axis=1)
            total = total + dot(g, w, 0, 1)
        out_ref[here] = total


def input_gradient(ids, gz, w_own, w_m, w_p, gs, waits=()):
    args = [gz, w_own, w_m, w_p, *gs]
    return pl.pallas_call(
        partial(input_kernel, tile=256),
        out_shape=jax.ShapeDtypeStruct(gz.shape, F32),
        grid_spec=pltpu.PrefetchScalarGridSpec(
            num_scalar_prefetch=1, grid=(1,),
            in_specs=[whole(a) for a in args] + [pl.BlockSpec(memory_space=pl.ANY) for _ in waits],
            out_specs=whole(gz)),
        compiler_params=params(20),
        cost_estimate=cost(7, 9_000_000),
        name="input_gradient",
    )(ids, *args, *waits)


def attention_kernel(ids, mine_near, mine_far, mate_near, mate_far, dwq_ref, dqb_ref, dwo_ref, dub_ref,
                     v0, v1, v2, v3, v4, v5, both):
    core, side = ids[0], ids[2]
    part = mine_near.shape[0]
    pair = dwo_ref.shape[0] // 2
    units = dub_ref.shape[1] // 2
    for c, near, far in ((core, mine_near, mine_far), (1 - core, mate_near, mate_far)):
        both[c, pl.ds(pl.multiple_of(side * part, 8), part)] = near[...].astype(F32)
        both[c, pl.ds(pl.multiple_of((1 - side) * part, 8), part)] = far[...].astype(F32)
    for m in range(2):
        cols = slice(m * pair, (m + 1) * pair)
        for c in range(3):
            dwq_ref[c, :, cols] = both[m, c * pair: (c + 1) * pair].T
        dwo_ref[cols] = both[m, 3 * pair: 4 * pair]
        dub_ref[:, m * units: (m + 1) * units] = both[m, 4 * pair: 4 * pair + 1]
        for c in range(2):
            dqb_ref[c: c + 1, cols] = both[m, 4 * pair + 1: 4 * pair + 2, c * pair: (c + 1) * pair]
    for k, ref in enumerate((v0, v1, v2, v3, v4, v5)):
        ref[...] = both[0, 4 * pair + 2 + k: 4 * pair + 3 + k]


def assemble_attention(ids, parts, pair, units):
    width = parts[0].shape[1]
    outs = [(3, width, 2 * pair), (2, 2 * pair), (2 * pair, width), (1, 2 * units)] + [(1, width)] * 6
    outs = tuple(jax.ShapeDtypeStruct(s, F32) for s in outs)
    return pl.pallas_call(
        attention_kernel,
        out_shape=outs,
        grid_spec=pltpu.PrefetchScalarGridSpec(
            num_scalar_prefetch=1, grid=(1,), in_specs=[whole(a) for a in parts],
            out_specs=tuple(whole(a) for a in outs),
            scratch_shapes=[pltpu.VMEM((2, 2 * parts[0].shape[0], width), F32)]),
        compiler_params=params(16),
        cost_estimate=cost(3, 4_000_000),
        name="assemble_attention",
    )(ids, *parts)


def dense_out_kernel(ids, mine_near, mine_far, mate_near, mate_far, dwu_ref, dwd_ref):
    core, side = ids[0], ids[2]
    units = mine_near.shape[1]
    part = mine_near.shape[0] // 2
    width = dwu_ref.shape[0]
    for c, near, far in ((core, mine_near, mine_far), (1 - core, mate_near, mate_far)):
        for s, ref in ((side, near), (1 - side, far)):
            dwu_ref[place(s, part), place(c, units)] = ref[:part].astype(F32)
            dwd_ref[pl.ds(pl.multiple_of(c * width + s * part, part), part)] = ref[part:].astype(F32)


def assemble_dense(ids, parts, units):
    width = parts[0].shape[1]
    outs = tuple(jax.ShapeDtypeStruct(s, F32) for s in ((width, 2 * units), (2 * units, width)))
    return pl.pallas_call(
        dense_out_kernel,
        out_shape=outs,
        grid_spec=pltpu.PrefetchScalarGridSpec(
            num_scalar_prefetch=1, grid=(1,), in_specs=[whole(a) for a in parts],
            out_specs=tuple(whole(a) for a in outs)),
        compiler_params=params(20),
        cost_estimate=cost(3, 6_000_000),
        name="assemble_dense",
    )(ids, *parts)


def send_tensor(a):
    n = lax.axis_size("tensor")
    return lax.ppermute(a, "tensor", [(i, (i + 1) % n) for i in range(n)])


def send_bit(a, bit):
    return lax.ppermute(a, "dp", [(i, i ^ (1 << bit)) for i in range(lax.axis_size("dp"))])


def plus(*members):
    return sum(m.astype(F32) for m in members).astype(BF)


def tie(*arrays):
    return lax.optimization_barrier(arrays)


def half_of(a, side, axis=0):
    n = a.shape[axis] // 2
    return lax.dynamic_slice_in_dim(a, side * n, n, axis)


def joined(mine, got, side, axis=0):
    return jnp.concatenate([jnp.where(side == 0, mine, got), jnp.where(side == 0, got, mine)], axis=axis)


def local(hidden_in, w_qkv, qv_bias, w_out, out_bias, gain1, shift1, w_up, up_bias, w_down,
          down_bias, gain2, shift2, lengths, head_perm, cotangent):
    rows, width = hidden_in.shape
    me = lax.axis_index("dp")
    core, xside, zside = me & 1, (me >> 1) & 1, (me >> 2) & 1
    upper_bits = list(range(3, lax.axis_size("dp").bit_length() - 1))
    pair = w_qkv.shape[2] // 2
    heads = head_perm.shape[0] // 2
    units = up_bias.shape[0] // 2
    row = lambda v: v.reshape(1, -1)
    ids = jnp.stack([core, lax.axis_index("tensor"), xside])

    def fetch(a, axis, rows_axis):
        sizes = list(a.shape)
        starts = [0] * a.ndim
        for dim, index in ((axis, core), (rows_axis, xside)):
            sizes[dim] //= 2
            starts[dim] += index * sizes[dim]
        return lax.dynamic_slice(a, starts, sizes)

    def forward(slot, w, bias, waits=()):
        return attend_forward(ids, lengths, head_perm if slot < 2 else perm_other, hidden_in, w, bias, slot, heads, pair, waits)

    perm_other, bias_other, ub_other = send_tensor(head_perm), send_tensor(qv_bias), send_tensor(up_bias)
    pieces = [fetch(w_qkv, 2, 1), fetch(w_up, 1, 0), fetch(w_down, 0, 0), fetch(w_out, 0, 0)]
    *pieces, perm_other, bias_other, ub_other = tie(*pieces, perm_other, bias_other, ub_other)
    wq_m, wu_m, wd_m, wo_m = (send_tensor(a) for a in pieces)
    kept = [forward(0, w_qkv, qv_bias, pieces)]
    wq_m, ctx = tie(wq_m, kept[0][3])
    wq_got = send_bit(wq_m, 1)
    kept.append(forward(1, w_qkv, qv_bias))
    wq_got, wu_m, ctx1 = tie(wq_got, wu_m, kept[1][3])
    wu_got = send_bit(wu_m, 1)
    wq_m = joined(wq_m, wq_got, xside, 1)
    wq_p = send_bit(wq_m, 0)
    kept.append(forward(2, wq_m, bias_other))
    wd_m, wo_m, wu_got, ctx2 = tie(wd_m, wo_m, wu_got, kept[2][3])
    wd_got, wo_got = send_bit(wd_m, 1), send_bit(wo_m, 1)
    wu_m = joined(wu_m, wu_got, xside)
    wu_p = send_bit(wu_m, 0)
    kept.append(forward(3, wq_p, bias_other))
    wd_got, wo_got, wu_p, ctx3 = tie(wd_got, wo_got, wu_p, kept[3][3])
    wd_m, wo_m = joined(wd_m, wd_got, xside), joined(wo_m, wo_got, xside)
    ctxs = [ctx, ctx1, ctx2, ctx3]
    wo_p, wd_p = send_bit(wo_m, 0), send_bit(wd_m, 0)
    out, g_z1, g_attn, ffn_m, ffn_p, smalls = dense(
        ids, lengths, hidden_in, cotangent, ctxs,
        [row(v) for v in (out_bias, gain1, shift1, down_bias, gain2, shift2)],
        [w_out, w_up, w_down, row(up_bias)], [wo_m, wu_m, wd_m, row(ub_other), wo_p, wu_p, wd_p])

    def backward(k, waits=()):
        if k < 2:
            perm, wo, block = head_perm, w_out, lambda c: c ^ k
        else:
            perm, wo, block = perm_other, (wo_m, wo_p)[k - 2], lambda c: 0
        return attend_backward(ids, perm, hidden_in, wo, block, kept[k], g_attn, smalls, k, waits)

    ffn_got = send_bit(ffn_p, 0)
    up = [(ffn_m[t, :width], ffn_got[t, :width]) for t in range(2)]
    down = [(ffn_m[t, width:], ffn_got[t, width:]) for t in range(2)]
    up_other = plus(*up[1])
    up_got = send_tensor(up_other)
    down_away = jnp.stack([plus(*[half_of(v, 1 - xside) for v in down[t]]) for t in range(2)])
    down_got = send_bit(down_away, 1)
    g3, d3 = backward(3, (up_other, down_away))
    d3_got = send_bit(d3, 0)
    g2, d2 = backward(2, (d3,))
    d2, up_got, down_got = tie(d2, up_got, down_got)
    up_away = plus(*[half_of(v, 1 - xside) for v in (*up[0], up_got)])
    down_other = plus(*[half_of(v, xside) for v in down[1]], down_got[1])
    up_got2 = send_bit(up_away, 1)
    down_got2 = send_tensor(down_other)
    other_away = plus(*[half_of(v, 1 - xside) for v in (d2, d3_got)])
    other_got = send_bit(other_away, 1)
    g1, d1 = backward(1, (up_away, down_other, other_away))
    d1_got = send_bit(d1, 0)
    d1, up_got2, down_got2 = tie(d1, up_got2, down_got2)
    ffn = jnp.concatenate([
        plus(*[half_of(v, xside) for v in (*up[0], up_got)], up_got2),
        plus(*[half_of(v, xside) for v in down[0]], down_got[0], down_got2)], axis=0)
    ffn_away = half_of(ffn, 1 - zside)
    ffn_got3 = send_bit(ffn_away, 2)
    ffn_away, other_got = tie(ffn_away, other_got)
    att_other = plus(*[half_of(v, xside) for v in (d2, d3_got)], other_got)
    att_got = send_tensor(att_other)
    g0, d0 = backward(0, (ffn_away, att_other))
    att_away = plus(*[half_of(v, 1 - xside) for v in (d0, d1_got)])
    att_got2 = send_bit(att_away, 1)
    att_away, ffn_got3 = tie(att_away, ffn_got3)
    ffn = plus(half_of(ffn, zside), ffn_got3)
    ffn_got4 = [send_bit(ffn, bit) for bit in upper_bits[:1]]
    ffn, att_got, att_got2 = tie(ffn, att_got, att_got2)
    att = plus(*[half_of(v, xside) for v in (d0, d1_got)], att_got, att_got2)
    att_got3 = send_bit(half_of(att, 1 - zside), 2)
    ffn = plus(ffn, *ffn_got4)
    for bit in upper_bits[1:]:
        ffn = plus(ffn, send_bit(ffn, bit))
    ffn_got5 = send_bit(ffn, 2)
    ffn, att_got3 = tie(ffn, att_got3)
    att = plus(half_of(att, zside), att_got3)
    att_got4 = [send_bit(att, bit) for bit in upper_bits[:1]]
    att, ffn_got5 = tie(att, ffn_got5)
    ffn = joined(ffn, ffn_got5, zside)
    ffn, *att_got4 = tie(ffn, *att_got4)
    att = plus(att, *att_got4)
    for bit in upper_bits[1:]:
        att = plus(att, send_bit(att, bit))
    att = joined(att, send_bit(att, 2), zside)
    ffn_far = send_bit(ffn, 1)
    att_far = send_bit(att, 1)
    x_grad = input_gradient(ids, g_z1, w_qkv, wq_m, wq_p, [g0, g1, g2, g3], (ffn, att))
    x_grad, ffn_far = tie(x_grad, ffn_far)
    d_wu, d_wd = assemble_dense(ids, [ffn, ffn_far, send_bit(ffn, 0), send_bit(ffn_far, 0)], units)
    d_wu, att_far = tie(d_wu, att_far)
    d_wq, d_qb, d_wo, d_ub, *vecs = assemble_attention(
        ids, [att, att_far, send_bit(att, 0), send_bit(att_far, 0)], pair, units)
    v = [a.reshape(-1) for a in vecs]
    return (out, x_grad, d_wq, d_qb, d_wo, v[0], v[1], v[2], d_wu, d_ub.reshape(-1), d_wd, v[3], v[4], v[5])


def solution(mesh):
    every = P()
    rows = P(("dp", "tensor"), None)
    return jax.shard_map(
        local,
        mesh=mesh,
        in_specs=(rows, P(None, None, "tensor"), P(None, "tensor"), P("tensor", None), every, every, every,
                  P(None, "tensor"), P("tensor"), P("tensor", None), every, every, every, P("dp"), P("tensor"), rows),
        out_specs=(rows, rows, P(None, None, "tensor"), P(None, "tensor"), P("tensor", None), every, every, every,
                   P(None, "tensor"), P("tensor"), P("tensor", None), every, every, every),
        check_vma=False,
    )
```

```python
import math
from functools import partial

import jax
import jax.numpy as jnp
from jax import lax
from jax.experimental import pallas as pl
from jax.experimental.pallas import tpu as pltpu
from jax.sharding import PartitionSpec as P

EPSILON = 1e-05
BF = jnp.bfloat16
F32 = jnp.float32
SMALL_ROWS = 64


def dot(a, b, ca, cb):
    return lax.dot_general(a, b, (((ca,), (cb,)), ((), ())), preferred_element_type=F32)


def place(index, size):
    return pl.ds(pl.multiple_of(index * size, size), size)


def whole(a):
    return pl.BlockSpec(a.shape, lambda *_: (0,) * len(a.shape))


def params(mebibytes):
    return pltpu.CompilerParams(vmem_limit_bytes=mebibytes * 1024 * 1024)


def cost(micros, size):
    return pl.CostEstimate(flops=int(micros * 1.1e9), bytes_accessed=size, transcendentals=0)


def forward_kernel(ids, lengths, perm, x_ref, w_ref, bias_ref, *rest, slot):
    qkv_ref, e_ref, inv_ref, ctx_ref = rest[-4:]
    width, rows = qkv_ref.shape[1:]
    half = rows // 2
    heads = e_ref.shape[1]
    size = width // heads
    quarter = ids[0] ^ (slot % 2)
    i = pl.program_id(0)

    @pl.when(i == 0)
    def _():
        every = dot(jnp.concatenate([w_ref[c] for c in range(3)], axis=1), x_ref[...], 0, 1)
        for c in range(3):
            part = every[c * width: (c + 1) * width]
            if c != 1:
                bias = bias_ref[c // 2: c // 2 + 1, place(quarter, width)]
                part = part + jnp.broadcast_to(bias, (width, width)).T[:, :1]
            qkv_ref[c] = part.astype(BF)

    mine = place(i, half)
    factor = math.log2(math.e) / math.sqrt(size)
    scores = []
    for h in range(heads):
        lanes = slice(h * size, (h + 1) * size)
        theirs = place(i ^ perm[quarter * heads + h], half)
        scores.append(dot(qkv_ref[1, lanes, theirs], qkv_ref[0, lanes, mine], 0, 0))
    for h in range(heads):
        lanes = slice(h * size, (h + 1) * size)
        j = i ^ perm[quarter * heads + h]
        theirs = place(j, half)
        s = scores[h]
        key = lax.broadcasted_iota(jnp.int32, (half, 1), 0) + j * half
        s = jnp.where(key < lengths[ids[1]], s, -1e30)
        top = jnp.max(s, axis=0, keepdims=True)
        e = jnp.exp2((s - top) * factor)
        inv = 1.0 / jnp.sum(e, axis=0, keepdims=True)
        low = e.astype(BF)
        e_ref[0, h] = low
        inv_ref[0, h] = inv
        ctx = dot(qkv_ref[2, lanes, theirs], low, 1, 0) * inv
        ctx_ref[lanes, mine] = ctx.astype(BF)


def attend_forward(ids, lengths, perm, x, w, bias, slot, heads, pair, waits=()):
    rows, width = x.shape
    half = rows // 2
    fixed = lambda *shape: pl.BlockSpec(shape, lambda i, *_: (0,) * len(shape))
    return pl.pallas_call(
        partial(forward_kernel, slot=slot),
        out_shape=(
            pltpu.HBM((3, pair, rows), BF),
            pltpu.HBM((2, heads, half, half), BF),
            pltpu.HBM((2, heads, 1, half), F32),
            pltpu.HBM((pair, rows), BF),
        ),
        grid_spec=pltpu.PrefetchScalarGridSpec(
            num_scalar_prefetch=3,
            grid=(2,),
            in_specs=[
                fixed(rows, width),
                pl.BlockSpec((3, width, pair), lambda i, s, *_: (0, 0, (s[0] ^ slot) if slot < 2 else 0)),
                fixed(*bias.shape),
                *[pl.BlockSpec(memory_space=pl.ANY) for _ in waits],
            ],
            out_specs=(
                fixed(3, pair, rows),
                pl.BlockSpec((1, heads, half, half), lambda i, *_: (i, 0, 0, 0)),
                pl.BlockSpec((1, heads, 1, half), lambda i, *_: (i, 0, 0, 0)),
                fixed(pair, rows),
            ),
        ),
        compiler_params=params(16),
        cost_estimate=cost(0.5, 400_000),
        name="attend_forward",
    )(ids, lengths, perm, x, w, bias, *waits)


def backward_kernel(ids, perm, x_ref, wo_ref, qkv_ref, e_ref, inv_ref, ctx_ref, ga_ref, small_ref, *rest, slot):
    g_out, dw_ref, gc_ref, g_ref, sem = rest[-5:]
    width, rows = gc_ref.shape
    half = rows // 2
    heads = e_ref.shape[1]
    size = width // heads
    quarter = ids[0] ^ (slot % 2)
    i = pl.program_id(0)

    @pl.when(i == 0)
    def _():
        gc_ref[...] = dot(wo_ref[...], ga_ref[...], 1, 1).astype(BF)
        dw_ref[3 * width: 4 * width] = dot(ctx_ref[...], ga_ref[...], 1, 0).astype(BF)

    mine = place(i, half)
    scaling = 1.0 / math.sqrt(size)
    for h in range(heads):
        lanes = slice(h * size, (h + 1) * size)
        j = i ^ perm[quarter * heads + h]
        theirs = place(j, half)
        g = gc_ref[lanes, mine].astype(F32) * inv_ref[0, h]
        inner = jnp.sum(g * ctx_ref[lanes, mine].astype(F32), axis=0, keepdims=True)
        g = g.astype(BF)
        e = e_ref[0, h]
        dp = dot(qkv_ref[2, lanes, theirs], g, 0, 0)
        ds = (e.astype(F32) * (dp - inner)).astype(BF)
        g_ref[2, lanes, theirs] = dot(g, e, 1, 1).astype(BF)
        g_ref[1, lanes, theirs] = (dot(qkv_ref[0, lanes, mine], ds, 1, 1) * scaling).astype(BF)
        g_ref[0, lanes, mine] = (dot(qkv_ref[1, lanes, theirs], ds, 1, 0) * scaling).astype(BF)

    @pl.when(i == 1)
    def _():
        copy = pltpu.make_async_copy(g_ref, g_out, sem)
        copy.start()
        small = small_ref[0]
        row = lax.broadcasted_iota(jnp.int32, small.shape, 0)
        dw_ref[:3 * width] = dot(g_ref[...].reshape(3 * width, rows), x_ref[...], 1, 0).astype(BF)
        ones = jnp.ones((8, rows), BF)
        sums = jnp.concatenate([dot(ones, g_ref[c], 1, 1) for c in (0, 2)] * 2, axis=1)
        small = jnp.where(row == 1, sums, small)
        small = jnp.concatenate([small, jnp.zeros((SMALL_ROWS - 8, small.shape[1]), F32)], axis=0)
        dw_ref[4 * width:] = small.astype(BF)
        copy.wait()


def attend_backward(ids, perm, x, wo, block, kept, g_attn, small, slot, waits=()):
    qkv, e, inv, ctx = kept
    rows, width = x.shape
    heads = e.shape[1]
    pair = ctx.shape[0]
    half = rows // 2
    fixed = lambda *shape: pl.BlockSpec(shape, lambda i, *_: (0,) * len(shape))
    return pl.pallas_call(
        partial(backward_kernel, slot=slot),
        out_shape=(
            pltpu.HBM((3, pair, rows), BF),
            jax.ShapeDtypeStruct((4 * pair + SMALL_ROWS, width), BF),
        ),
        grid_spec=pltpu.PrefetchScalarGridSpec(
            num_scalar_prefetch=2,
            grid=(2,),
            in_specs=[
                fixed(rows, width),
                pl.BlockSpec((pair, width), lambda i, s, p: (block(s[0]), 0)),
                fixed(3, pair, rows),
                pl.BlockSpec((1, heads, half, half), lambda i, *_: (i, 0, 0, 0)),
                pl.BlockSpec((1, heads, 1, half), lambda i, *_: (i, 0, 0, 0)),
                fixed(pair, rows),
                fixed(rows, width),
                pl.BlockSpec((1, 8, width), lambda i, *_: (slot, 0, 0)),
                *[pl.BlockSpec(memory_space=pl.ANY) for _ in waits],
            ],
            out_specs=(pl.BlockSpec(memory_space=pl.ANY), fixed(4 * pair + SMALL_ROWS, width)),
            scratch_shapes=[pltpu.VMEM((pair, rows), BF), pltpu.VMEM((3, pair, rows), BF), pltpu.SemaphoreType.DMA],
        ),
        compiler_params=params(16),
        cost_estimate=cost(7.8, 4_000_000),
        name="attend_backward",
    )(ids, perm, x, wo, qkv, e, inv, ctx, g_attn, small, *waits)


def normed(v):
    centre = v - jnp.mean(v, axis=-1, keepdims=True)
    inv = lax.rsqrt(jnp.mean(centre * centre, axis=-1, keepdims=True) + EPSILON)
    return centre * inv, inv


def norm_back(g, hat, inv, gain):
    g = g * gain
    return (g - jnp.mean(g, axis=-1, keepdims=True) - hat * jnp.mean(g * hat, axis=-1, keepdims=True)) * inv


def gelu_parts(v):
    t = 1.0 / (1.0 + (0.3275911 * math.sqrt(0.5)) * jnp.abs(v))
    bell = jnp.exp2(v * v * (-0.5 * math.log2(math.e)))
    poly = ((((0.5 * 1.061405429 * t - 0.5 * 1.453152027) * t + 0.5 * 1.421413741) * t
             - 0.5 * 0.284496736) * t + 0.5 * 0.254829592) * t
    tail = poly * bell
    cdf = jnp.where(v < 0, tail, 1.0 - tail)
    return v * cdf, cdf + v * bell * (1.0 / math.sqrt(2.0 * math.pi))


def dense_kernel(ids, lengths, x_ref, cot_ref, c0, c1, c2, c3, out_bias, gain1, shift1, down_bias, gain2, shift2,
                 wo_own, wu_own, wd_own, ub_own, wo_m, wu_m, wd_m, ub_other, wo_p, wu_p, wd_p,
                 out_to, gz_to, ga_to, gm_to, gp_to, small_ref,
                 out_ref, gz_ref, ga_ref, gw_ref, wo_all, n1_all, gf_all, act_all, gp_all, sems, tile):
    rows, width = x_ref.shape
    pair = c0.shape[0]
    units = ub_own.shape[1] // 2
    core, length = ids[0], lengths[ids[1]]

    wo_all[0:pair] = wo_own[place(core, pair)]
    wo_all[pair: 2 * pair] = wo_own[place(1 - core, pair)]
    wo_all[2 * pair: 3 * pair] = wo_m[...]
    wo_all[3 * pair:] = wo_p[...]
    near, far = place(core, units), place(1 - core, units)
    ups = [wu_own.at[:, near], wu_own.at[:, far], wu_m, wu_p]
    downs = [wd_own.at[near], wd_own.at[far], wd_m, wd_p]
    biases = [ub_own.at[:, near], ub_own.at[:, far],
              ub_other.at[:, near], ub_other.at[:, far]]
    small_ref[...] = jnp.zeros_like(small_ref)
    copies = []

    def send(source, target):
        copies.append(pltpu.make_async_copy(source, target, sems.at[len(copies)]))
        copies[-1].start()

    for r in range(rows // tile):
        here = slice(r * tile, (r + 1) * tile)
        ctx = jnp.concatenate([c[:, here] for c in (c0, c1, c2, c3)], axis=0)
        z1 = x_ref[here].astype(F32) + dot(ctx, wo_all[...], 0, 0) + out_bias[...]
        hat1, inv1 = normed(z1)
        n1 = hat1 * gain1[...] + shift1[...]
        low = n1.astype(BF)
        n1_all[here] = low
        z2 = n1 + down_bias[...]
        for k in range(4):
            cols = slice(k * units, (k + 1) * units)
            act, slope = gelu_parts(dot(low, ups[k][...], 1, 0) + biases[k][...])
            act = act.astype(BF)
            act_all[here, cols] = act
            gp_all[here, cols] = slope.astype(BF)
            z2 = z2 + dot(act, downs[k][...], 1, 0)
        hat2, inv2 = normed(z2)
        row = lax.broadcasted_iota(jnp.int32, (tile, 1), 0) + r * tile
        valid = (row < length).astype(F32)
        out_ref[here] = ((hat2 * gain2[...] + shift2[...]) * valid).astype(BF)
        g_out = cot_ref[here].astype(F32) * valid
        g_z2 = norm_back(g_out, hat2, inv2, gain2[...])
        g_ffn = g_z2.astype(BF)
        gf_all[here] = g_ffn
        g_n1 = g_z2
        for k in range(4):
            cols = slice(k * units, (k + 1) * units)
            g_pre = (dot(g_ffn, downs[k][...], 1, 1) * gp_all[here, cols].astype(F32)).astype(BF)
            gp_all[here, cols] = g_pre
            small_ref[k, 0:1] += jnp.sum(g_pre.astype(F32), axis=0, keepdims=True)
            g_n1 = g_n1 + dot(g_pre, ups[k][...], 1, 1)
        g_z1 = norm_back(g_n1, hat1, inv1, gain1[...])
        gz_ref[here] = g_z1
        g_attn = g_z1.astype(BF)
        ga_ref[here] = g_attn
        sums = (g_attn.astype(F32), g_n1 * hat1, g_n1, g_ffn.astype(F32), g_out * hat2, g_out)
        for k, v in enumerate(sums):
            small_ref[0, 2 + k: 3 + k] += jnp.sum(v, axis=0, keepdims=True)
        for source, target in ((gz_ref, gz_to), (ga_ref, ga_to), (out_ref, out_to)):
            send(source.at[here], target.at[here])

    for k in range(1, 4):
        small_ref[k, 2:8] = small_ref[0, 2:8]
    flipped = n1_all[...].T
    for k in (1, 3, 0, 2):
        cols = slice(k * units, (k + 1) * units)
        to = gw_ref.at[k]
        to[:width] = dot(flipped, gp_all[:, cols], 1, 0).astype(BF)
        to[width:] = dot(act_all[:, cols], gf_all[...], 0, 0).astype(BF)
        send(to, (gm_to, gp_to)[k % 2].at[k // 2])
    for copy in copies:
        copy.wait()


def dense(ids, lengths, x, cot, ctxs, vecs, own, other):
    rows, width = x.shape
    pair = ctxs[0].shape[0]
    units = own[3].shape[1] // 2
    args = [x, cot, *ctxs, *vecs, *own, *other]
    tile = 512
    outs = (
        pltpu.HBM((rows, width), BF),
        pltpu.HBM((rows, width), F32),
        pltpu.HBM((rows, width), BF),
        pltpu.HBM((2, width + units, width), BF),
        pltpu.HBM((2, width + units, width), BF),
        jax.ShapeDtypeStruct((4, 8, width), F32),
    )
    return pl.pallas_call(
        partial(dense_kernel, tile=tile),
        out_shape=outs,
        grid_spec=pltpu.PrefetchScalarGridSpec(
            num_scalar_prefetch=2,
            grid=(1,),
            in_specs=[whole(a) for a in args],
            out_specs=(pl.BlockSpec(memory_space=pl.ANY),) * 5 + (whole(outs[5]),),
            scratch_shapes=[
                pltpu.VMEM((rows, width), BF),
                pltpu.VMEM((rows, width), F32),
                pltpu.VMEM((rows, width), BF),
                pltpu.VMEM((4, width + units, width), BF),
                pltpu.VMEM((4 * pair, width), BF),
                pltpu.VMEM((rows, width), BF),
                pltpu.VMEM((rows, width), BF),
                pltpu.VMEM((rows, 4 * units), BF),
                pltpu.VMEM((rows, 4 * units), BF),
                pltpu.SemaphoreType.DMA((3 * (rows // tile) + 4,)),
            ],
        ),
        compiler_params=params(36),
        cost_estimate=cost(31, 20_000_000),
        name="dense",
    )(ids, lengths, *args)


def input_kernel(ids, gz_ref, w_own, w_m, w_p, g0, g1, g2, g3, *rest, tile):
    out_ref = rest[-1]
    rows, width = gz_ref.shape
    pair = g0.shape[1]
    core = ids[0]

    @pl.loop(0, rows // tile)
    def _(r):
        here = place(r, tile)
        total = gz_ref[here]
        for c in range(3):
            g = jnp.concatenate([g0[c, :, here], g1[c, :, here], g2[c, :, here], g3[c, :, here]], axis=0)
            w = jnp.concatenate([w_own[c, :, place(core, pair)], w_own[c, :, place(1 - core, pair)], w_m[c], w_p[c]], axis=1)
            total = total + dot(g, w, 0, 1)
        out_ref[here] = total


def input_gradient(ids, gz, w_own, w_m, w_p, gs, waits=()):
    args = [gz, w_own, w_m, w_p, *gs]
    return pl.pallas_call(
        partial(input_kernel, tile=256),
        out_shape=jax.ShapeDtypeStruct(gz.shape, F32),
        grid_spec=pltpu.PrefetchScalarGridSpec(
            num_scalar_prefetch=1, grid=(1,),
            in_specs=[whole(a) for a in args] + [pl.BlockSpec(memory_space=pl.ANY) for _ in waits],
            out_specs=whole(gz)),
        compiler_params=params(20),
        cost_estimate=cost(7, 9_000_000),
        name="input_gradient",
    )(ids, *args, *waits)


def attention_kernel(ids, mine_near, mine_far, mate_near, mate_far, dwq_ref, dqb_ref, dwo_ref, dub_ref,
                     v0, v1, v2, v3, v4, v5, both):
    core, side = ids[0], ids[2]
    part = mine_near.shape[0]
    pair = dwo_ref.shape[0] // 2
    units = dub_ref.shape[1] // 2
    for c, near, far in ((core, mine_near, mine_far), (1 - core, mate_near, mate_far)):
        both[c, pl.ds(pl.multiple_of(side * part, 8), part)] = near[...].astype(F32)
        both[c, pl.ds(pl.multiple_of((1 - side) * part, 8), part)] = far[...].astype(F32)
    for m in range(2):
        cols = slice(m * pair, (m + 1) * pair)
        for c in range(3):
            dwq_ref[c, :, cols] = both[m, c * pair: (c + 1) * pair].T
        dwo_ref[cols] = both[m, 3 * pair: 4 * pair]
        dub_ref[:, m * units: (m + 1) * units] = both[m, 4 * pair: 4 * pair + 1]
        for c in range(2):
            dqb_ref[c: c + 1, cols] = both[m, 4 * pair + 1: 4 * pair + 2, c * pair: (c + 1) * pair]
    for k, ref in enumerate((v0, v1, v2, v3, v4, v5)):
        ref[...] = both[0, 4 * pair + 2 + k: 4 * pair + 3 + k]


def assemble_attention(ids, parts, pair, units):
    width = parts[0].shape[1]
    outs = [(3, width, 2 * pair), (2, 2 * pair), (2 * pair, width), (1, 2 * units)] + [(1, width)] * 6
    outs = tuple(jax.ShapeDtypeStruct(s, F32) for s in outs)
    return pl.pallas_call(
        attention_kernel,
        out_shape=outs,
        grid_spec=pltpu.PrefetchScalarGridSpec(
            num_scalar_prefetch=1, grid=(1,), in_specs=[whole(a) for a in parts],
            out_specs=tuple(whole(a) for a in outs),
            scratch_shapes=[pltpu.VMEM((2, 2 * parts[0].shape[0], width), F32)]),
        compiler_params=params(16),
        cost_estimate=cost(3, 4_000_000),
        name="assemble_attention",
    )(ids, *parts)


def dense_out_kernel(ids, mine_near, mine_far, mate_near, mate_far, dwu_ref, dwd_ref):
    core, side = ids[0], ids[2]
    units = mine_near.shape[1]
    part = mine_near.shape[0] // 2
    width = dwu_ref.shape[0]
    for c, near, far in ((core, mine_near, mine_far), (1 - core, mate_near, mate_far)):
        for s, ref in ((side, near), (1 - side, far)):
            dwu_ref[place(s, part), place(c, units)] = ref[:part].astype(F32)
            dwd_ref[pl.ds(pl.multiple_of(c * width + s * part, part), part)] = ref[part:].astype(F32)


def assemble_dense(ids, parts, units):
    width = parts[0].shape[1]
    outs = tuple(jax.ShapeDtypeStruct(s, F32) for s in ((width, 2 * units), (2 * units, width)))
    return pl.pallas_call(
        dense_out_kernel,
        out_shape=outs,
        grid_spec=pltpu.PrefetchScalarGridSpec(
            num_scalar_prefetch=1, grid=(1,), in_specs=[whole(a) for a in parts],
            out_specs=tuple(whole(a) for a in outs)),
        compiler_params=params(20),
        cost_estimate=cost(3, 6_000_000),
        name="assemble_dense",
    )(ids, *parts)


def send_tensor(a):
    n = lax.axis_size("tensor")
    return lax.ppermute(a, "tensor", [(i, (i + 1) % n) for i in range(n)])


def send_bit(a, bit):
    return lax.ppermute(a, "dp", [(i, i ^ (1 << bit)) for i in range(lax.axis_size("dp"))])


def plus(*members):
    return sum(m.astype(F32) for m in members).astype(BF)


def tie(*arrays):
    return lax.optimization_barrier(arrays)


def half_of(a, side, axis=0):
    n = a.shape[axis] // 2
    return lax.dynamic_slice_in_dim(a, side * n, n, axis)


def joined(mine, got, side, axis=0):
    return jnp.concatenate([jnp.where(side == 0, mine, got), jnp.where(side == 0, got, mine)], axis=axis)


def local(hidden_in, w_qkv, qv_bias, w_out, out_bias, gain1, shift1, w_up, up_bias, w_down,
          down_bias, gain2, shift2, lengths, head_perm, cotangent):
    rows, width = hidden_in.shape
    me = lax.axis_index("dp")
    core, xside, zside = me & 1, (me >> 1) & 1, (me >> 2) & 1
    upper_bits = list(range(3, lax.axis_size("dp").bit_length() - 1))
    pair = w_qkv.shape[2] // 2
    heads = head_perm.shape[0] // 2
    units = up_bias.shape[0] // 2
    row = lambda v: v.reshape(1, -1)
    ids = jnp.stack([core, lax.axis_index("tensor"), xside])

    def fetch(a, axis, rows_axis):
        sizes = list(a.shape)
        starts = [0] * a.ndim
        for dim, index in ((axis, core), (rows_axis, xside)):
            sizes[dim] //= 2
            starts[dim] += index * sizes[dim]
        return lax.dynamic_slice(a, starts, sizes)

    def forward(slot, w, bias, waits=()):
        return attend_forward(ids, lengths, head_perm if slot < 2 else perm_other, hidden_in, w, bias, slot, heads, pair, waits)

    perm_other, bias_other, ub_other = send_tensor(head_perm), send_tensor(qv_bias), send_tensor(up_bias)
    pieces = [fetch(w_qkv, 2, 1), fetch(w_up, 1, 0), fetch(w_down, 0, 0), fetch(w_out, 0, 0)]
    *pieces, perm_other, bias_other, ub_other = tie(*pieces, perm_other, bias_other, ub_other)
    wq_m, wu_m, wd_m, wo_m = (send_tensor(a) for a in pieces)
    kept = [forward(0, w_qkv, qv_bias, pieces)]
    wq_m, ctx = tie(wq_m, kept[0][3])
    wq_got = send_bit(wq_m, 1)
    kept.append(forward(1, w_qkv, qv_bias))
    wq_got, wu_m, ctx1 = tie(wq_got, wu_m, kept[1][3])
    wu_got = send_bit(wu_m, 1)
    wq_m = joined(wq_m, wq_got, xside, 1)
    wq_p = send_bit(wq_m, 0)
    kept.append(forward(2, wq_m, bias_other))
    wd_m, wo_m, wu_got, ctx2 = tie(wd_m, wo_m, wu_got, kept[2][3])
    wd_got, wo_got = send_bit(wd_m, 1), send_bit(wo_m, 1)
    wu_m = joined(wu_m, wu_got, xside)
    wu_p = send_bit(wu_m, 0)
    kept.append(forward(3, wq_p, bias_other))
    wd_got, wo_got, wu_p, ctx3 = tie(wd_got, wo_got, wu_p, kept[3][3])
    wd_m, wo_m = joined(wd_m, wd_got, xside), joined(wo_m, wo_got, xside)
    ctxs = [ctx, ctx1, ctx2, ctx3]
    wo_p, wd_p = send_bit(wo_m, 0), send_bit(wd_m, 0)
    out, g_z1, g_attn, ffn_m, ffn_p, smalls = dense(
        ids, lengths, hidden_in, cotangent, ctxs,
        [row(v) for v in (out_bias, gain1, shift1, down_bias, gain2, shift2)],
        [w_out, w_up, w_down, row(up_bias)], [wo_m, wu_m, wd_m, row(ub_other), wo_p, wu_p, wd_p])

    def backward(k, waits=()):
        if k < 2:
            perm, wo, block = head_perm, w_out, lambda c: c ^ k
        else:
            perm, wo, block = perm_other, (wo_m, wo_p)[k - 2], lambda c: 0
        return attend_backward(ids, perm, hidden_in, wo, block, kept[k], g_attn, smalls, k, waits)

    ffn_got = send_bit(ffn_p, 0)
    up = [(ffn_m[t, :width], ffn_got[t, :width]) for t in range(2)]
    down = [(ffn_m[t, width:], ffn_got[t, width:]) for t in range(2)]
    up_other = plus(*up[1])
    up_got = send_tensor(up_other)
    down_away = jnp.stack([plus(*[half_of(v, 1 - xside) for v in down[t]]) for t in range(2)])
    down_got = send_bit(down_away, 1)
    g3, d3 = backward(3, (up_other, down_away))
    d3_got = send_bit(d3, 0)
    g2, d2 = backward(2, (d3,))
    d2, up_got, down_got = tie(d2, up_got, down_got)
    up_away = plus(*[half_of(v, 1 - xside) for v in (*up[0], up_got)])
    down_other = plus(*[half_of(v, xside) for v in down[1]], down_got[1])
    up_got2 = send_bit(up_away, 1)
    down_got2 = send_tensor(down_other)
    other_away = plus(*[half_of(v, 1 - xside) for v in (d2, d3_got)])
    other_got = send_bit(other_away, 1)
    g1, d1 = backward(1, (up_away, down_other, other_away))
    d1_got = send_bit(d1, 0)
    d1, up_got2, down_got2 = tie(d1, up_got2, down_got2)
    ffn = jnp.concatenate([
        plus(*[half_of(v, xside) for v in (*up[0], up_got)], up_got2),
        plus(*[half_of(v, xside) for v in down[0]], down_got[0], down_got2)], axis=0)
    ffn_away = half_of(ffn, 1 - zside)
    ffn_got3 = send_bit(ffn_away, 2)
    ffn_away, other_got = tie(ffn_away, other_got)
    att_other = plus(*[half_of(v, xside) for v in (d2, d3_got)], other_got)
    att_got = send_tensor(att_other)
    g0, d0 = backward(0, (ffn_away, att_other))
    att_away = plus(*[half_of(v, 1 - xside) for v in (d0, d1_got)])
    att_got2 = send_bit(att_away, 1)
    att_away, ffn_got3 = tie(att_away, ffn_got3)
    ffn = plus(half_of(ffn, zside), ffn_got3)
    ffn_got4 = [send_bit(ffn, bit) for bit in upper_bits[:1]]
    ffn, att_got, att_got2 = tie(ffn, att_got, att_got2)
    att = plus(*[half_of(v, xside) for v in (d0, d1_got)], att_got, att_got2)
    att_got3 = send_bit(half_of(att, 1 - zside), 2)
    ffn = plus(ffn, *ffn_got4)
    for bit in upper_bits[1:]:
        ffn = plus(ffn, send_bit(ffn, bit))
    ffn_got5 = send_bit(ffn, 2)
    ffn, att_got3 = tie(ffn, att_got3)
    att = plus(half_of(att, zside), att_got3)
    att_got4 = [send_bit(att, bit) for bit in upper_bits[:1]]
    att, ffn_got5 = tie(att, ffn_got5)
    ffn = joined(ffn, ffn_got5, zside)
    ffn, *att_got4 = tie(ffn, *att_got4)
    att = plus(att, *att_got4)
    for bit in upper_bits[1:]:
        att = plus(att, send_bit(att, bit))
    att = joined(att, send_bit(att, 2), zside)
    ffn_far = send_bit(ffn, 1)
    att_far = send_bit(att, 1)
    x_grad = input_gradient(ids, g_z1, w_qkv, wq_m, wq_p, [g0, g1, g2, g3], (ffn, att))
    x_grad, ffn_far = tie(x_grad, ffn_far)
    d_wu, d_wd = assemble_dense(ids, [ffn, ffn_far, send_bit(ffn, 0), send_bit(ffn_far, 0)], units)
    d_wu, att_far = tie(d_wu, att_far)
    d_wq, d_qb, d_wo, d_ub, *vecs = assemble_attention(
        ids, [att, att_far, send_bit(att, 0), send_bit(att_far, 0)], pair, units)
    v = [a.reshape(-1) for a in vecs]
    return (out, x_grad, d_wq, d_qb, d_wo, v[0], v[1], v[2], d_wu, d_ub.reshape(-1), d_wd, v[3], v[4], v[5])


def solution(mesh):
    every = P()
    rows = P(("dp", "tensor"), None)
    return jax.shard_map(
        local,
        mesh=mesh,
        in_specs=(rows, P(None, None, "tensor"), P(None, "tensor"), P("tensor", None), every, every, every,
                  P(None, "tensor"), P("tensor"), P("tensor", None), every, every, every, P("dp"), P("tensor"), rows),
        out_specs=(rows, rows, P(None, None, "tensor"), P(None, "tensor"), P("tensor", None), every, every, every,
                   P(None, "tensor"), P("tensor"), P("tensor", None), every, every, every),
        check_vma=False,
    )
```

```python
import math
from functools import partial

import jax
import jax.numpy as jnp
from jax import lax
from jax.experimental import pallas as pl
from jax.experimental.pallas import tpu as pltpu
from jax.sharding import PartitionSpec as P

EPSILON = 1e-05
BF = jnp.bfloat16
F32 = jnp.float32
SMALL_ROWS = 64


def dot(a, b, ca, cb):
    return lax.dot_general(a, b, (((ca,), (cb,)), ((), ())), preferred_element_type=F32)


def place(index, size):
    return pl.ds(pl.multiple_of(index * size, size), size)


def whole(a):
    return pl.BlockSpec(a.shape, lambda *_: (0,) * len(a.shape))


def params(mebibytes):
    return pltpu.CompilerParams(vmem_limit_bytes=mebibytes * 1024 * 1024)


def cost(micros, size):
    return pl.CostEstimate(flops=int(micros * 1.1e9), bytes_accessed=size, transcendentals=0)


def forward_kernel(ids, lengths, perm, x_ref, w_ref, bias_ref, *rest, slot):
    qkv_ref, e_ref, inv_ref, ctx_ref = rest[-4:]
    width, rows = qkv_ref.shape[1:]
    half = rows // 2
    heads = e_ref.shape[1]
    size = width // heads
    quarter = ids[0] ^ (slot % 2)
    i = pl.program_id(0)

    @pl.when(i == 0)
    def _():
        every = dot(jnp.concatenate([w_ref[c] for c in range(3)], axis=1), x_ref[...], 0, 1)
        for c in range(3):
            part = every[c * width: (c + 1) * width]
            if c != 1:
                bias = bias_ref[c // 2: c // 2 + 1, place(quarter, width)]
                part = part + jnp.broadcast_to(bias, (width, width)).T[:, :1]
            qkv_ref[c] = part.astype(BF)

    mine = place(i, half)
    factor = math.log2(math.e) / math.sqrt(size)
    scores = []
    for h in range(heads):
        lanes = slice(h * size, (h + 1) * size)
        theirs = place(i ^ perm[quarter * heads + h], half)
        scores.append(dot(qkv_ref[1, lanes, theirs], qkv_ref[0, lanes, mine], 0, 0))
    for h in range(heads):
        lanes = slice(h * size, (h + 1) * size)
        j = i ^ perm[quarter * heads + h]
        theirs = place(j, half)
        s = scores[h]
        key = lax.broadcasted_iota(jnp.int32, (half, 1), 0) + j * half
        s = jnp.where(key < lengths[ids[1]], s, -1e30)
        top = jnp.max(s, axis=0, keepdims=True)
        e = jnp.exp2((s - top) * factor)
        inv = 1.0 / jnp.sum(e, axis=0, keepdims=True)
        low = e.astype(BF)
        e_ref[0, h] = low
        inv_ref[0, h] = inv
        ctx = dot(qkv_ref[2, lanes, theirs], low, 1, 0) * inv
        ctx_ref[lanes, mine] = ctx.astype(BF)


def attend_forward(ids, lengths, perm, x, w, bias, slot, heads, pair, waits=()):
    rows, width = x.shape
    half = rows // 2
    fixed = lambda *shape: pl.BlockSpec(shape, lambda i, *_: (0,) * len(shape))
    return pl.pallas_call(
        partial(forward_kernel, slot=slot),
        out_shape=(
            pltpu.HBM((3, pair, rows), BF),
            pltpu.HBM((2, heads, half, half), BF),
            pltpu.HBM((2, heads, 1, half), F32),
            pltpu.HBM((pair, rows), BF),
        ),
        grid_spec=pltpu.PrefetchScalarGridSpec(
            num_scalar_prefetch=3,
            grid=(2,),
            in_specs=[
                fixed(rows, width),
                pl.BlockSpec((3, width, pair), lambda i, s, *_: (0, 0, (s[0] ^ slot) if slot < 2 else 0)),
                fixed(*bias.shape),
                *[pl.BlockSpec(memory_space=pl.ANY) for _ in waits],
            ],
            out_specs=(
                fixed(3, pair, rows),
                pl.BlockSpec((1, heads, half, half), lambda i, *_: (i, 0, 0, 0)),
                pl.BlockSpec((1, heads, 1, half), lambda i, *_: (i, 0, 0, 0)),
                fixed(pair, rows),
            ),
        ),
        compiler_params=params(16),
        cost_estimate=cost(0.5, 400_000),
        name="attend_forward",
    )(ids, lengths, perm, x, w, bias, *waits)


def backward_kernel(ids, perm, x_ref, wo_ref, qkv_ref, e_ref, inv_ref, ctx_ref, ga_ref, small_ref, *rest, slot):
    g_out, dw_ref, gc_ref, g_ref, sem = rest[-5:]
    width, rows = gc_ref.shape
    half = rows // 2
    heads = e_ref.shape[1]
    size = width // heads
    quarter = ids[0] ^ (slot % 2)
    i = pl.program_id(0)

    @pl.when(i == 0)
    def _():
        gc_ref[...] = dot(wo_ref[...], ga_ref[...], 1, 1).astype(BF)
        dw_ref[3 * width: 4 * width] = dot(ctx_ref[...], ga_ref[...], 1, 0).astype(BF)

    mine = place(i, half)
    scaling = 1.0 / math.sqrt(size)
    for h in range(heads):
        lanes = slice(h * size, (h + 1) * size)
        j = i ^ perm[quarter * heads + h]
        theirs = place(j, half)
        g = gc_ref[lanes, mine].astype(F32) * inv_ref[0, h]
        inner = jnp.sum(g * ctx_ref[lanes, mine].astype(F32), axis=0, keepdims=True)
        g = g.astype(BF)
        e = e_ref[0, h]
        dp = dot(qkv_ref[2, lanes, theirs], g, 0, 0)
        ds = (e.astype(F32) * (dp - inner)).astype(BF)
        g_ref[2, lanes, theirs] = dot(g, e, 1, 1).astype(BF)
        g_ref[1, lanes, theirs] = (dot(qkv_ref[0, lanes, mine], ds, 1, 1) * scaling).astype(BF)
        g_ref[0, lanes, mine] = (dot(qkv_ref[1, lanes, theirs], ds, 1, 0) * scaling).astype(BF)

    @pl.when(i == 1)
    def _():
        copy = pltpu.make_async_copy(g_ref, g_out, sem)
        copy.start()
        small = small_ref[0]
        row = lax.broadcasted_iota(jnp.int32, small.shape, 0)
        dw_ref[:3 * width] = dot(g_ref[...].reshape(3 * width, rows), x_ref[...], 1, 0).astype(BF)
        ones = jnp.ones((8, rows), BF)
        sums = jnp.concatenate([dot(ones, g_ref[c], 1, 1) for c in (0, 2)] * 2, axis=1)
        small = jnp.where(row == 1, sums, small)
        small = jnp.concatenate([small, jnp.zeros((SMALL_ROWS - 8, small.shape[1]), F32)], axis=0)
        dw_ref[4 * width:] = small.astype(BF)
        copy.wait()


def attend_backward(ids, perm, x, wo, block, kept, g_attn, small, slot, waits=()):
    qkv, e, inv, ctx = kept
    rows, width = x.shape
    heads = e.shape[1]
    pair = ctx.shape[0]
    half = rows // 2
    fixed = lambda *shape: pl.BlockSpec(shape, lambda i, *_: (0,) * len(shape))
    return pl.pallas_call(
        partial(backward_kernel, slot=slot),
        out_shape=(
            pltpu.HBM((3, pair, rows), BF),
            jax.ShapeDtypeStruct((4 * pair + SMALL_ROWS, width), BF),
        ),
        grid_spec=pltpu.PrefetchScalarGridSpec(
            num_scalar_prefetch=2,
            grid=(2,),
            in_specs=[
                fixed(rows, width),
                pl.BlockSpec((pair, width), lambda i, s, p: (block(s[0]), 0)),
                fixed(3, pair, rows),
                pl.BlockSpec((1, heads, half, half), lambda i, *_: (i, 0, 0, 0)),
                pl.BlockSpec((1, heads, 1, half), lambda i, *_: (i, 0, 0, 0)),
                fixed(pair, rows),
                fixed(rows, width),
                pl.BlockSpec((1, 8, width), lambda i, *_: (slot, 0, 0)),
                *[pl.BlockSpec(memory_space=pl.ANY) for _ in waits],
            ],
            out_specs=(pl.BlockSpec(memory_space=pl.ANY), fixed(4 * pair + SMALL_ROWS, width)),
            scratch_shapes=[pltpu.VMEM((pair, rows), BF), pltpu.VMEM((3, pair, rows), BF), pltpu.SemaphoreType.DMA],
        ),
        compiler_params=params(16),
        cost_estimate=cost(7.8, 4_000_000),
        name="attend_backward",
    )(ids, perm, x, wo, qkv, e, inv, ctx, g_attn, small, *waits)


def normed(v):
    centre = v - jnp.mean(v, axis=-1, keepdims=True)
    inv = lax.rsqrt(jnp.mean(centre * centre, axis=-1, keepdims=True) + EPSILON)
    return centre * inv, inv


def norm_back(g, hat, inv, gain):
    g = g * gain
    return (g - jnp.mean(g, axis=-1, keepdims=True) - hat * jnp.mean(g * hat, axis=-1, keepdims=True)) * inv


def gelu_parts(v):
    t = 1.0 / (1.0 + (0.3275911 * math.sqrt(0.5)) * jnp.abs(v))
    bell = jnp.exp2(v * v * (-0.5 * math.log2(math.e)))
    poly = ((((0.5 * 1.061405429 * t - 0.5 * 1.453152027) * t + 0.5 * 1.421413741) * t
             - 0.5 * 0.284496736) * t + 0.5 * 0.254829592) * t
    tail = poly * bell
    cdf = jnp.where(v < 0, tail, 1.0 - tail)
    return v * cdf, cdf + v * bell * (1.0 / math.sqrt(2.0 * math.pi))


def dense_kernel(ids, lengths, x_ref, cot_ref, c0, c1, c2, c3, out_bias, gain1, shift1, down_bias, gain2, shift2,
                 wo_own, wu_own, wd_own, ub_own, wo_m, wu_m, wd_m, ub_other, wo_p, wu_p, wd_p,
                 out_to, gz_to, ga_to, *rest, tile):
    (small_ref, out_ref, gz_ref, ga_ref, gw_ref, wo_all, n1_all, gf_all, act_all, gp_all, sems) = rest[8:]
    rows, width = x_ref.shape
    pair = c0.shape[0]
    units = ub_own.shape[1] // 2
    core, length = ids[0], lengths[ids[1]]

    wo_all[0:pair] = wo_own[place(core, pair)]
    wo_all[pair: 2 * pair] = wo_own[place(1 - core, pair)]
    wo_all[2 * pair: 3 * pair] = wo_m[...]
    wo_all[3 * pair:] = wo_p[...]
    near, far = place(core, units), place(1 - core, units)
    ups = [wu_own.at[:, near], wu_own.at[:, far], wu_m, wu_p]
    downs = [wd_own.at[near], wd_own.at[far], wd_m, wd_p]
    biases = [ub_own.at[:, near], ub_own.at[:, far],
              ub_other.at[:, near], ub_other.at[:, far]]
    small_ref[...] = jnp.zeros_like(small_ref)
    copies = []

    def send(source, target):
        copies.append(pltpu.make_async_copy(source, target, sems.at[len(copies)]))
        copies[-1].start()

    for r in range(rows // tile):
        here = slice(r * tile, (r + 1) * tile)
        ctx = jnp.concatenate([c[:, here] for c in (c0, c1, c2, c3)], axis=0)
        z1 = x_ref[here].astype(F32) + dot(ctx, wo_all[...], 0, 0) + out_bias[...]
        hat1, inv1 = normed(z1)
        n1 = hat1 * gain1[...] + shift1[...]
        low = n1.astype(BF)
        n1_all[here] = low
        z2 = n1 + down_bias[...]
        for k in range(4):
            cols = slice(k * units, (k + 1) * units)
            act, slope = gelu_parts(dot(low, ups[k][...], 1, 0) + biases[k][...])
            act = act.astype(BF)
            act_all[here, cols] = act
            gp_all[here, cols] = slope.astype(BF)
            z2 = z2 + dot(act, downs[k][...], 1, 0)
        hat2, inv2 = normed(z2)
        row = lax.broadcasted_iota(jnp.int32, (tile, 1), 0) + r * tile
        valid = (row < length).astype(F32)
        out_ref[here] = ((hat2 * gain2[...] + shift2[...]) * valid).astype(BF)
        g_out = cot_ref[here].astype(F32) * valid
        g_z2 = norm_back(g_out, hat2, inv2, gain2[...])
        g_ffn = g_z2.astype(BF)
        gf_all[here] = g_ffn
        g_n1 = g_z2
        for k in range(4):
            cols = slice(k * units, (k + 1) * units)
            g_pre = (dot(g_ffn, downs[k][...], 1, 1) * gp_all[here, cols].astype(F32)).astype(BF)
            gp_all[here, cols] = g_pre
            small_ref[k, 0:1] += jnp.sum(g_pre.astype(F32), axis=0, keepdims=True)
            g_n1 = g_n1 + dot(g_pre, ups[k][...], 1, 1)
        g_z1 = norm_back(g_n1, hat1, inv1, gain1[...])
        gz_ref[here] = g_z1
        g_attn = g_z1.astype(BF)
        ga_ref[here] = g_attn
        sums = (g_attn.astype(F32), g_n1 * hat1, g_n1, g_ffn.astype(F32), g_out * hat2, g_out)
        for k, v in enumerate(sums):
            small_ref[0, 2 + k: 3 + k] += jnp.sum(v, axis=0, keepdims=True)
        for source, target in ((gz_ref, gz_to), (ga_ref, ga_to), (out_ref, out_to)):
            send(source.at[here], target.at[here])

    for k in range(1, 4):
        small_ref[k, 2:8] = small_ref[0, 2:8]
    flipped = n1_all[...].T
    for k in (3, 1, 2, 0):
        cols = slice(k * units, (k + 1) * units)
        gw_ref[2 * k] = dot(flipped, gp_all[:, cols], 1, 0).astype(BF)
        send(gw_ref.at[2 * k], rest[2 * k])
        gw_ref[2 * k + 1] = dot(act_all[:, cols], gf_all[...], 0, 0).astype(BF)
        send(gw_ref.at[2 * k + 1], rest[2 * k + 1])
    for copy in copies:
        copy.wait()


def dense(ids, lengths, x, cot, ctxs, vecs, own, other):
    rows, width = x.shape
    pair = ctxs[0].shape[0]
    units = own[3].shape[1] // 2
    args = [x, cot, *ctxs, *vecs, *own, *other]
    tile = 512
    outs = (
        pltpu.HBM((rows, width), BF),
        pltpu.HBM((rows, width), F32),
        pltpu.HBM((rows, width), BF),
        *[pltpu.HBM((width, units) if n % 2 == 0 else (units, width), BF) for n in range(8)],
        jax.ShapeDtypeStruct((4, 8, width), F32),
    )
    return pl.pallas_call(
        partial(dense_kernel, tile=tile),
        out_shape=outs,
        grid_spec=pltpu.PrefetchScalarGridSpec(
            num_scalar_prefetch=2,
            grid=(1,),
            in_specs=[whole(a) for a in args],
            out_specs=(pl.BlockSpec(memory_space=pl.ANY),) * 11 + (whole(outs[11]),),
            scratch_shapes=[
                pltpu.VMEM((rows, width), BF),
                pltpu.VMEM((rows, width), F32),
                pltpu.VMEM((rows, width), BF),
                pltpu.VMEM((8, width, units), BF),
                pltpu.VMEM((4 * pair, width), BF),
                pltpu.VMEM((rows, width), BF),
                pltpu.VMEM((rows, width), BF),
                pltpu.VMEM((rows, 4 * units), BF),
                pltpu.VMEM((rows, 4 * units), BF),
                pltpu.SemaphoreType.DMA((3 * (rows // tile) + 8,)),
            ],
        ),
        compiler_params=params(36),
        cost_estimate=cost(31, 20_000_000),
        name="dense",
    )(ids, lengths, *args)


def input_kernel(ids, gz_ref, w_own, w_m, w_p, g0, g1, g2, g3, *rest, tile):
    out_ref = rest[-1]
    rows, width = gz_ref.shape
    pair = g0.shape[1]
    core = ids[0]

    @pl.loop(0, rows // tile)
    def _(r):
        here = place(r, tile)
        total = gz_ref[here]
        for c in range(3):
            g = jnp.concatenate([g0[c, :, here], g1[c, :, here], g2[c, :, here], g3[c, :, here]], axis=0)
            w = jnp.concatenate([w_own[c, :, place(core, pair)], w_own[c, :, place(1 - core, pair)], w_m[c], w_p[c]], axis=1)
            total = total + dot(g, w, 0, 1)
        out_ref[here] = total


def input_gradient(ids, gz, w_own, w_m, w_p, gs, waits=()):
    args = [gz, w_own, w_m, w_p, *gs]
    return pl.pallas_call(
        partial(input_kernel, tile=256),
        out_shape=jax.ShapeDtypeStruct(gz.shape, F32),
        grid_spec=pltpu.PrefetchScalarGridSpec(
            num_scalar_prefetch=1, grid=(1,),
            in_specs=[whole(a) for a in args] + [pl.BlockSpec(memory_space=pl.ANY) for _ in waits],
            out_specs=whole(gz)),
        compiler_params=params(20),
        cost_estimate=cost(7, 9_000_000),
        name="input_gradient",
    )(ids, *args, *waits)


def attention_kernel(ids, mine_near, mine_far, mate_near, mate_far, dwq_ref, dqb_ref, dwo_ref, dub_ref,
                     v0, v1, v2, v3, v4, v5, both):
    core, side = ids[0], ids[2]
    part = mine_near.shape[0]
    pair = dwo_ref.shape[0] // 2
    units = dub_ref.shape[1] // 2
    for c, near, far in ((core, mine_near, mine_far), (1 - core, mate_near, mate_far)):
        both[c, pl.ds(pl.multiple_of(side * part, 8), part)] = near[...].astype(F32)
        both[c, pl.ds(pl.multiple_of((1 - side) * part, 8), part)] = far[...].astype(F32)
    for m in range(2):
        cols = slice(m * pair, (m + 1) * pair)
        for c in range(3):
            dwq_ref[c, :, cols] = both[m, c * pair: (c + 1) * pair].T
        dwo_ref[cols] = both[m, 3 * pair: 4 * pair]
        dub_ref[:, m * units: (m + 1) * units] = both[m, 4 * pair: 4 * pair + 1]
        for c in range(2):
            dqb_ref[c: c + 1, cols] = both[m, 4 * pair + 1: 4 * pair + 2, c * pair: (c + 1) * pair]
    for k, ref in enumerate((v0, v1, v2, v3, v4, v5)):
        ref[...] = both[0, 4 * pair + 2 + k: 4 * pair + 3 + k]


def assemble_attention(ids, parts, pair, units):
    width = parts[0].shape[1]
    outs = [(3, width, 2 * pair), (2, 2 * pair), (2 * pair, width), (1, 2 * units)] + [(1, width)] * 6
    outs = tuple(jax.ShapeDtypeStruct(s, F32) for s in outs)
    return pl.pallas_call(
        attention_kernel,
        out_shape=outs,
        grid_spec=pltpu.PrefetchScalarGridSpec(
            num_scalar_prefetch=1, grid=(1,), in_specs=[whole(a) for a in parts],
            out_specs=tuple(whole(a) for a in outs),
            scratch_shapes=[pltpu.VMEM((2, 2 * parts[0].shape[0], width), F32)]),
        compiler_params=params(16),
        cost_estimate=cost(3, 4_000_000),
        name="assemble_attention",
    )(ids, *parts)


def dense_out_kernel(ids, mine_near, mine_far, mate_near, mate_far, dwu_ref, dwd_ref):
    core, side = ids[0], ids[2]
    units = mine_near.shape[1]
    part = mine_near.shape[0] // 2
    width = dwu_ref.shape[0]
    for c, near, far in ((core, mine_near, mine_far), (1 - core, mate_near, mate_far)):
        for s, ref in ((side, near), (1 - side, far)):
            dwu_ref[place(s, part), place(c, units)] = ref[:part].astype(F32)
            dwd_ref[pl.ds(pl.multiple_of(c * width + s * part, part), part)] = ref[part:].astype(F32)


def assemble_dense(ids, parts, units):
    width = parts[0].shape[1]
    outs = tuple(jax.ShapeDtypeStruct(s, F32) for s in ((width, 2 * units), (2 * units, width)))
    return pl.pallas_call(
        dense_out_kernel,
        out_shape=outs,
        grid_spec=pltpu.PrefetchScalarGridSpec(
            num_scalar_prefetch=1, grid=(1,), in_specs=[whole(a) for a in parts],
            out_specs=tuple(whole(a) for a in outs)),
        compiler_params=params(20),
        cost_estimate=cost(3, 6_000_000),
        name="assemble_dense",
    )(ids, *parts)


def cut_kernel(ids, wq, wu, wd, wo, q_out, u_out, d_out, o_out, ids_out):
    for n in range(3):
        ids_out[n] = ids[n]
    for source, target in ((wq, q_out), (wu, u_out), (wd, d_out), (wo, o_out)):
        target[...] = source[...]


def cut_weights(ids, wq, wu, wd, wo):
    shapes = [(3, wq.shape[1] // 2, wq.shape[2] // 2), (wu.shape[0] // 2, wu.shape[1] // 2),
              (wd.shape[0] // 4, wd.shape[1]), (wo.shape[0] // 4, wo.shape[1])]
    spots = [lambda i, s: (0, s[2], s[0]), lambda i, s: (s[2], s[0]),
             lambda i, s: (2 * s[0] + s[2], 0), lambda i, s: (2 * s[0] + s[2], 0)]
    outs = [jax.ShapeDtypeStruct(a, BF) for a in shapes]
    return pl.pallas_call(
        cut_kernel,
        out_shape=(*outs, jax.ShapeDtypeStruct(ids.shape, jnp.int32)),
        grid_spec=pltpu.PrefetchScalarGridSpec(
            num_scalar_prefetch=1, grid=(1,),
            in_specs=[pl.BlockSpec(a, spot) for a, spot in zip(shapes, spots)],
            out_specs=(*[whole(a) for a in outs], pl.BlockSpec(memory_space=pltpu.SMEM))),
        compiler_params=params(8),
        cost_estimate=cost(1, 2_000_000),
        name="cut_weights",
    )(ids, *[pltpu.with_memory_space_constraint(a, pltpu.HBM) for a in (wq, wu, wd, wo)])


def send_tensor(a):
    n = lax.axis_size("tensor")
    return lax.ppermute(a, "tensor", [(i, (i + 1) % n) for i in range(n)])


def send_bit(a, bit):
    return lax.ppermute(a, "dp", [(i, i ^ (1 << bit)) for i in range(lax.axis_size("dp"))])


def plus(*members):
    return sum(m.astype(F32) for m in members).astype(BF)


def tie(*arrays):
    return lax.optimization_barrier(arrays)


def half_of(a, side, axis=0):
    n = a.shape[axis] // 2
    return lax.dynamic_slice_in_dim(a, side * n, n, axis)


def joined(mine, got, side, axis=0):
    return jnp.concatenate([jnp.where(side == 0, mine, got), jnp.where(side == 0, got, mine)], axis=axis)


def local(hidden_in, w_qkv, qv_bias, w_out, out_bias, gain1, shift1, w_up, up_bias, w_down,
          down_bias, gain2, shift2, lengths, head_perm, cotangent):
    rows, width = hidden_in.shape
    me = lax.axis_index("dp")
    core, xside, zside = me & 1, (me >> 1) & 1, (me >> 2) & 1
    upper_bits = list(range(3, lax.axis_size("dp").bit_length() - 1))
    pair = w_qkv.shape[2] // 2
    heads = head_perm.shape[0] // 2
    units = up_bias.shape[0] // 2
    row = lambda v: v.reshape(1, -1)
    ids = jnp.stack([core, lax.axis_index("tensor"), xside])

    def forward(slot, w, bias, waits=()):
        return attend_forward(ids, lengths, head_perm if slot < 2 else perm_other, hidden_in, w, bias, slot, heads, pair, waits)

    perm_other, bias_other, ub_other = send_tensor(head_perm), send_tensor(qv_bias), send_tensor(up_bias)
    *pieces, ids = cut_weights(ids, w_qkv, w_up, w_down, w_out)
    *pieces, perm_other, bias_other, ub_other = tie(*pieces, perm_other, bias_other, ub_other)
    wq_m, wu_m, wd_m, wo_m = (send_tensor(a) for a in pieces)
    kept = [forward(0, w_qkv, qv_bias)]
    wq_m, ctx = tie(wq_m, kept[0][3])
    wq_got = send_bit(wq_m, 1)
    kept.append(forward(1, w_qkv, qv_bias))
    wq_got, wu_m, ctx1 = tie(wq_got, wu_m, kept[1][3])
    wu_got = send_bit(wu_m, 1)
    wq_m = joined(wq_m, wq_got, xside, 1)
    wq_p = send_bit(wq_m, 0)
    kept.append(forward(2, wq_m, bias_other))
    wd_m, wo_m, wu_got, ctx2 = tie(wd_m, wo_m, wu_got, kept[2][3])
    wd_got, wo_got = send_bit(wd_m, 1), send_bit(wo_m, 1)
    wu_m = joined(wu_m, wu_got, xside)
    wu_p = send_bit(wu_m, 0)
    kept.append(forward(3, wq_p, bias_other))
    wd_got, wo_got, wu_p, ctx3 = tie(wd_got, wo_got, wu_p, kept[3][3])
    wd_m, wo_m = joined(wd_m, wd_got, xside), joined(wo_m, wo_got, xside)
    ctxs = [ctx, ctx1, ctx2, ctx3]
    wo_p, wd_p = send_bit(wo_m, 0), send_bit(wd_m, 0)
    out, g_z1, g_attn, *ffn, smalls = dense(
        ids, lengths, hidden_in, cotangent, ctxs,
        [row(v) for v in (out_bias, gain1, shift1, down_bias, gain2, shift2)],
        [w_out, w_up, w_down, row(up_bias)], [wo_m, wu_m, wd_m, row(ub_other), wo_p, wu_p, wd_p])

    def backward(k, waits=()):
        if k < 2:
            perm, wo, block = head_perm, w_out, lambda c: c ^ k
        else:
            perm, wo, block = perm_other, (wo_m, wo_p)[k - 2], lambda c: 0
        return attend_backward(ids, perm, hidden_in, wo, block, kept[k], g_attn, smalls, k, waits)

    crossed = {n: send_bit(ffn[n], 0) for n in (6, 7, 3, 2)}
    up = [(ffn[4 * t], crossed[4 * t + 2]) for t in range(2)]
    down = [(ffn[4 * t + 1], crossed[4 * t + 3]) for t in range(2)]
    up_other = plus(*up[1])
    up_got = send_tensor(up_other)
    down_away = jnp.stack([plus(*[half_of(v, 1 - xside) for v in down[t]]) for t in range(2)])
    down_got = send_bit(down_away, 1)
    g3, d3 = backward(3, (up_other, down_away))
    d3_got = send_bit(d3, 0)
    g2, d2 = backward(2, (d3,))
    d2, up_got, down_got = tie(d2, up_got, down_got)
    up_away = plus(*[half_of(v, 1 - xside) for v in (*up[0], up_got)])
    down_other = plus(*[half_of(v, xside) for v in down[1]], down_got[1])
    up_got2 = send_bit(up_away, 1)
    down_got2 = send_tensor(down_other)
    other_away = plus(*[half_of(v, 1 - xside) for v in (d2, d3_got)])
    other_got = send_bit(other_away, 1)
    g1, d1 = backward(1, (up_away, down_other, other_away))
    d1_got = send_bit(d1, 0)
    d1, up_got2, down_got2 = tie(d1, up_got2, down_got2)
    ffn = jnp.concatenate([
        plus(*[half_of(v, xside) for v in (*up[0], up_got)], up_got2),
        plus(*[half_of(v, xside) for v in down[0]], down_got[0], down_got2)], axis=0)
    ffn_away = half_of(ffn, 1 - zside)
    ffn_got3 = send_bit(ffn_away, 2)
    ffn_away, other_got = tie(ffn_away, other_got)
    att_other = plus(*[half_of(v, xside) for v in (d2, d3_got)], other_got)
    att_got = send_tensor(att_other)
    g0, d0 = backward(0, (ffn_away, att_other))
    att_away = plus(*[half_of(v, 1 - xside) for v in (d0, d1_got)])
    att_got2 = send_bit(att_away, 1)
    att_away, ffn_got3 = tie(att_away, ffn_got3)
    ffn = plus(half_of(ffn, zside), ffn_got3)
    ffn_got4 = [send_bit(ffn, bit) for bit in upper_bits[:1]]
    ffn, att_got, att_got2 = tie(ffn, att_got, att_got2)
    att = plus(*[half_of(v, xside) for v in (d0, d1_got)], att_got, att_got2)
    att_got3 = send_bit(half_of(att, 1 - zside), 2)
    ffn = plus(ffn, *ffn_got4)
    for bit in upper_bits[1:]:
        ffn = plus(ffn, send_bit(ffn, bit))
    ffn_got5 = send_bit(ffn, 2)
    ffn, att_got3 = tie(ffn, att_got3)
    att = plus(half_of(att, zside), att_got3)
    att_got4 = [send_bit(att, bit) for bit in upper_bits[:1]]
    att, ffn_got5 = tie(att, ffn_got5)
    ffn = joined(ffn, ffn_got5, zside)
    ffn, *att_got4 = tie(ffn, *att_got4)
    att = plus(att, *att_got4)
    for bit in upper_bits[1:]:
        att = plus(att, send_bit(att, bit))
    att = joined(att, send_bit(att, 2), zside)
    ffn_far = send_bit(ffn, 1)
    att_far = send_bit(att, 1)
    x_grad = input_gradient(ids, g_z1, w_qkv, wq_m, wq_p, [g0, g1, g2, g3], (ffn, att))
    x_grad, ffn_far = tie(x_grad, ffn_far)
    d_wu, d_wd = assemble_dense(ids, [ffn, ffn_far, send_bit(ffn, 0), send_bit(ffn_far, 0)], units)
    d_wu, att_far = tie(d_wu, att_far)
    d_wq, d_qb, d_wo, d_ub, *vecs = assemble_attention(
        ids, [att, att_far, send_bit(att, 0), send_bit(att_far, 0)], pair, units)
    v = [a.reshape(-1) for a in vecs]
    return (out, x_grad, d_wq, d_qb, d_wo, v[0], v[1], v[2], d_wu, d_ub.reshape(-1), d_wd, v[3], v[4], v[5])


def solution(mesh):
    every = P()
    rows = P(("dp", "tensor"), None)
    return jax.shard_map(
        local,
        mesh=mesh,
        in_specs=(rows, P(None, None, "tensor"), P(None, "tensor"), P("tensor", None), every, every, every,
                  P(None, "tensor"), P("tensor"), P("tensor", None), every, every, every, P("dp"), P("tensor"), rows),
        out_specs=(rows, rows, P(None, None, "tensor"), P(None, "tensor"), P("tensor", None), every, every, every,
                   P(None, "tensor"), P("tensor"), P("tensor", None), every, every, every),
        check_vma=False,
    )
```

```python
import math
from functools import partial

import jax
import jax.numpy as jnp
from jax import lax
from jax.experimental import pallas as pl
from jax.experimental.pallas import tpu as pltpu
from jax.sharding import PartitionSpec as P

EPSILON = 1e-05
BF = jnp.bfloat16
F32 = jnp.float32
SMALL_ROWS = 64


def dot(a, b, ca, cb):
    return lax.dot_general(a, b, (((ca,), (cb,)), ((), ())), preferred_element_type=F32)


def place(index, size):
    return pl.ds(pl.multiple_of(index * size, size), size)


def whole(a):
    return pl.BlockSpec(a.shape, lambda *_: (0,) * len(a.shape))


def params(mebibytes):
    return pltpu.CompilerParams(vmem_limit_bytes=mebibytes * 1024 * 1024)


def cost(micros, size):
    return pl.CostEstimate(flops=int(micros * 1.1e9), bytes_accessed=size, transcendentals=0)


def forward_kernel(ids, lengths, perm, x_ref, w_ref, bias_ref, *rest, slot):
    qkv_ref, e_ref, inv_ref, ctx_ref = rest[-4:]
    width, rows = qkv_ref.shape[1:]
    half = rows // 2
    heads = e_ref.shape[1]
    size = width // heads
    quarter = ids[0] ^ (slot % 2)
    i = pl.program_id(0)

    @pl.when(i == 0)
    def _():
        every = dot(jnp.concatenate([w_ref[c] for c in range(3)], axis=1), x_ref[...], 0, 1)
        for c in range(3):
            part = every[c * width: (c + 1) * width]
            if c != 1:
                bias = bias_ref[c // 2: c // 2 + 1, place(quarter, width)]
                part = part + jnp.broadcast_to(bias, (width, width)).T[:, :1]
            qkv_ref[c] = part.astype(BF)

    mine = place(i, half)
    factor = math.log2(math.e) / math.sqrt(size)
    scores = []
    for h in range(heads):
        lanes = slice(h * size, (h + 1) * size)
        theirs = place(i ^ perm[quarter * heads + h], half)
        scores.append(dot(qkv_ref[1, lanes, theirs], qkv_ref[0, lanes, mine], 0, 0))
    for h in range(heads):
        lanes = slice(h * size, (h + 1) * size)
        j = i ^ perm[quarter * heads + h]
        theirs = place(j, half)
        s = scores[h]
        key = lax.broadcasted_iota(jnp.int32, (half, 1), 0) + j * half
        s = jnp.where(key < lengths[ids[1]], s, -1e30)
        top = jnp.max(s, axis=0, keepdims=True)
        e = jnp.exp2((s - top) * factor)
        inv = 1.0 / jnp.sum(e, axis=0, keepdims=True)
        low = e.astype(BF)
        e_ref[0, h] = low
        inv_ref[0, h] = inv
        ctx = dot(qkv_ref[2, lanes, theirs], low, 1, 0) * inv
        ctx_ref[lanes, mine] = ctx.astype(BF)


def attend_forward(ids, lengths, perm, x, w, bias, slot, heads, pair, waits=()):
    rows, width = x.shape
    half = rows // 2
    fixed = lambda *shape: pl.BlockSpec(shape, lambda i, *_: (0,) * len(shape))
    return pl.pallas_call(
        partial(forward_kernel, slot=slot),
        out_shape=(
            pltpu.HBM((3, pair, rows), BF),
            pltpu.HBM((2, heads, half, half), BF),
            pltpu.HBM((2, heads, 1, half), F32),
            pltpu.HBM((pair, rows), BF),
        ),
        grid_spec=pltpu.PrefetchScalarGridSpec(
            num_scalar_prefetch=3,
            grid=(2,),
            in_specs=[
                fixed(rows, width),
                pl.BlockSpec((3, width, pair), lambda i, s, *_: (0, 0, (s[0] ^ slot) if slot < 2 else 0)),
                fixed(*bias.shape),
                *[pl.BlockSpec(memory_space=pl.ANY) for _ in waits],
            ],
            out_specs=(
                fixed(3, pair, rows),
                pl.BlockSpec((1, heads, half, half), lambda i, *_: (i, 0, 0, 0)),
                pl.BlockSpec((1, heads, 1, half), lambda i, *_: (i, 0, 0, 0)),
                fixed(pair, rows),
            ),
        ),
        compiler_params=params(16),
        cost_estimate=cost(0.5, 400_000),
        name="attend_forward",
    )(ids, lengths, perm, x, w, bias, *waits)


def backward_kernel(ids, perm, x_ref, wo_ref, qkv_ref, e_ref, inv_ref, ctx_ref, ga_ref, small_ref, *rest, slot):
    g_out, dw_ref, gc_ref, g_ref, sem = rest[-5:]
    width, rows = gc_ref.shape
    half = rows // 2
    heads = e_ref.shape[1]
    size = width // heads
    quarter = ids[0] ^ (slot % 2)
    i = pl.program_id(0)

    @pl.when(i == 0)
    def _():
        gc_ref[...] = dot(wo_ref[...], ga_ref[...], 1, 1).astype(BF)
        dw_ref[3 * width: 4 * width] = dot(ctx_ref[...], ga_ref[...], 1, 0).astype(BF)

    mine = place(i, half)
    scaling = 1.0 / math.sqrt(size)
    for h in range(heads):
        lanes = slice(h * size, (h + 1) * size)
        j = i ^ perm[quarter * heads + h]
        theirs = place(j, half)
        g = gc_ref[lanes, mine].astype(F32) * inv_ref[0, h]
        inner = jnp.sum(g * ctx_ref[lanes, mine].astype(F32), axis=0, keepdims=True)
        g = g.astype(BF)
        e = e_ref[0, h]
        dp = dot(qkv_ref[2, lanes, theirs], g, 0, 0)
        ds = (e.astype(F32) * (dp - inner)).astype(BF)
        g_ref[2, lanes, theirs] = dot(g, e, 1, 1).astype(BF)
        g_ref[1, lanes, theirs] = (dot(qkv_ref[0, lanes, mine], ds, 1, 1) * scaling).astype(BF)
        g_ref[0, lanes, mine] = (dot(qkv_ref[1, lanes, theirs], ds, 1, 0) * scaling).astype(BF)

    @pl.when(i == 1)
    def _():
        copy = pltpu.make_async_copy(g_ref, g_out, sem)
        copy.start()
        small = small_ref[0]
        row = lax.broadcasted_iota(jnp.int32, small.shape, 0)
        dw_ref[:3 * width] = dot(g_ref[...].reshape(3 * width, rows), x_ref[...], 1, 0).astype(BF)
        ones = jnp.ones((8, rows), BF)
        sums = jnp.concatenate([dot(ones, g_ref[c], 1, 1) for c in (0, 2)] * 2, axis=1)
        small = jnp.where(row == 1, sums, small)
        small = jnp.concatenate([small, jnp.zeros((SMALL_ROWS - 8, small.shape[1]), F32)], axis=0)
        dw_ref[4 * width:] = small.astype(BF)
        copy.wait()


def attend_backward(ids, perm, x, wo, block, kept, g_attn, small, slot, waits=()):
    qkv, e, inv, ctx = kept
    rows, width = x.shape
    heads = e.shape[1]
    pair = ctx.shape[0]
    half = rows // 2
    fixed = lambda *shape: pl.BlockSpec(shape, lambda i, *_: (0,) * len(shape))
    return pl.pallas_call(
        partial(backward_kernel, slot=slot),
        out_shape=(
            pltpu.HBM((3, pair, rows), BF),
            jax.ShapeDtypeStruct((4 * pair + SMALL_ROWS, width), BF),
        ),
        grid_spec=pltpu.PrefetchScalarGridSpec(
            num_scalar_prefetch=2,
            grid=(2,),
            in_specs=[
                fixed(rows, width),
                pl.BlockSpec((pair, width), lambda i, s, p: (block(s[0]), 0)),
                fixed(3, pair, rows),
                pl.BlockSpec((1, heads, half, half), lambda i, *_: (i, 0, 0, 0)),
                pl.BlockSpec((1, heads, 1, half), lambda i, *_: (i, 0, 0, 0)),
                fixed(pair, rows),
                fixed(rows, width),
                pl.BlockSpec((1, 8, width), lambda i, *_: (slot, 0, 0)),
                *[pl.BlockSpec(memory_space=pl.ANY) for _ in waits],
            ],
            out_specs=(pl.BlockSpec(memory_space=pl.ANY), fixed(4 * pair + SMALL_ROWS, width)),
            scratch_shapes=[pltpu.VMEM((pair, rows), BF), pltpu.VMEM((3, pair, rows), BF), pltpu.SemaphoreType.DMA],
        ),
        compiler_params=params(16),
        cost_estimate=cost(7.8, 4_000_000),
        name="attend_backward",
    )(ids, perm, x, wo, qkv, e, inv, ctx, g_attn, small, *waits)


def normed(v):
    centre = v - jnp.mean(v, axis=-1, keepdims=True)
    inv = lax.rsqrt(jnp.mean(centre * centre, axis=-1, keepdims=True) + EPSILON)
    return centre * inv, inv


def norm_back(g, hat, inv, gain):
    g = g * gain
    return (g - jnp.mean(g, axis=-1, keepdims=True) - hat * jnp.mean(g * hat, axis=-1, keepdims=True)) * inv


def gelu_parts(v):
    t = 1.0 / (1.0 + (0.3275911 * math.sqrt(0.5)) * jnp.abs(v))
    bell = jnp.exp2(v * v * (-0.5 * math.log2(math.e)))
    poly = ((((0.5 * 1.061405429 * t - 0.5 * 1.453152027) * t + 0.5 * 1.421413741) * t
             - 0.5 * 0.284496736) * t + 0.5 * 0.254829592) * t
    tail = poly * bell
    cdf = jnp.where(v < 0, tail, 1.0 - tail)
    return v * cdf, cdf + v * bell * (1.0 / math.sqrt(2.0 * math.pi))


def dense_kernel(ids, lengths, x_ref, cot_ref, c0, c1, c2, c3, out_bias, gain1, shift1, down_bias, gain2, shift2,
                 wo_own, wu_own, wd_own, ub_own, wo_m, wu_m, wd_m, ub_other, wo_p, wu_p, wd_p,
                 out_to, gz_to, ga_to, *rest, tile):
    (small_ref, out_ref, gz_ref, ga_ref, gw_ref, wo_all, n1_all, gf_all, act_all, gp_all, sems) = rest[8:]
    rows, width = x_ref.shape
    pair = c0.shape[0]
    units = ub_own.shape[1] // 2
    core, length = ids[0], lengths[ids[1]]

    wo_all[0:pair] = wo_own[place(core, pair)]
    wo_all[pair: 2 * pair] = wo_own[place(1 - core, pair)]
    wo_all[2 * pair: 3 * pair] = wo_m[...]
    wo_all[3 * pair:] = wo_p[...]
    near, far = place(core, units), place(1 - core, units)
    ups = [wu_own.at[:, near], wu_own.at[:, far], wu_m, wu_p]
    downs = [wd_own.at[near], wd_own.at[far], wd_m, wd_p]
    biases = [ub_own.at[:, near], ub_own.at[:, far],
              ub_other.at[:, near], ub_other.at[:, far]]
    small_ref[...] = jnp.zeros_like(small_ref)
    copies = []

    def send(source, target):
        copies.append(pltpu.make_async_copy(source, target, sems.at[len(copies)]))
        copies[-1].start()

    for r in range(rows // tile):
        here = slice(r * tile, (r + 1) * tile)
        ctx = jnp.concatenate([c[:, here] for c in (c0, c1, c2, c3)], axis=0)
        z1 = x_ref[here].astype(F32) + dot(ctx, wo_all[...], 0, 0) + out_bias[...]
        hat1, inv1 = normed(z1)
        n1 = hat1 * gain1[...] + shift1[...]
        low = n1.astype(BF)
        n1_all[here] = low
        z2 = n1 + down_bias[...]
        for k in range(4):
            cols = slice(k * units, (k + 1) * units)
            act, slope = gelu_parts(dot(low, ups[k][...], 1, 0) + biases[k][...])
            act = act.astype(BF)
            act_all[here, cols] = act
            gp_all[here, cols] = slope.astype(BF)
            z2 = z2 + dot(act, downs[k][...], 1, 0)
        hat2, inv2 = normed(z2)
        row = lax.broadcasted_iota(jnp.int32, (tile, 1), 0) + r * tile
        valid = (row < length).astype(F32)
        out_ref[here] = ((hat2 * gain2[...] + shift2[...]) * valid).astype(BF)
        g_out = cot_ref[here].astype(F32) * valid
        g_z2 = norm_back(g_out, hat2, inv2, gain2[...])
        g_ffn = g_z2.astype(BF)
        gf_all[here] = g_ffn
        g_n1 = g_z2
        for k in range(4):
            cols = slice(k * units, (k + 1) * units)
            g_pre = (dot(g_ffn, downs[k][...], 1, 1) * gp_all[here, cols].astype(F32)).astype(BF)
            gp_all[here, cols] = g_pre
            small_ref[k, 0:1] += jnp.sum(g_pre.astype(F32), axis=0, keepdims=True)
            g_n1 = g_n1 + dot(g_pre, ups[k][...], 1, 1)
        g_z1 = norm_back(g_n1, hat1, inv1, gain1[...])
        gz_ref[here] = g_z1
        g_attn = g_z1.astype(BF)
        ga_ref[here] = g_attn
        sums = (g_attn.astype(F32), g_n1 * hat1, g_n1, g_ffn.astype(F32), g_out * hat2, g_out)
        for k, v in enumerate(sums):
            small_ref[0, 2 + k: 3 + k] += jnp.sum(v, axis=0, keepdims=True)
        for source, target in ((gz_ref, gz_to), (ga_ref, ga_to), (out_ref, out_to)):
            send(source.at[here], target.at[here])

    for k in range(1, 4):
        small_ref[k, 2:8] = small_ref[0, 2:8]
    flipped = n1_all[...].T
    for k in (3, 1, 2, 0):
        cols = slice(k * units, (k + 1) * units)
        gw_ref[2 * k] = dot(flipped, gp_all[:, cols], 1, 0).astype(BF)
        send(gw_ref.at[2 * k], rest[2 * k])
        gw_ref[2 * k + 1] = dot(act_all[:, cols], gf_all[...], 0, 0).astype(BF)
        send(gw_ref.at[2 * k + 1], rest[2 * k + 1])
    for copy in copies:
        copy.wait()


def dense(ids, lengths, x, cot, ctxs, vecs, own, other):
    rows, width = x.shape
    pair = ctxs[0].shape[0]
    units = own[3].shape[1] // 2
    args = [x, cot, *ctxs, *vecs, *own, *other]
    tile = 512
    outs = (
        pltpu.HBM((rows, width), BF),
        pltpu.HBM((rows, width), F32),
        pltpu.HBM((rows, width), BF),
        *[pltpu.HBM((width, units) if n % 2 == 0 else (units, width), BF) for n in range(8)],
        jax.ShapeDtypeStruct((4, 8, width), F32),
    )
    return pl.pallas_call(
        partial(dense_kernel, tile=tile),
        out_shape=outs,
        grid_spec=pltpu.PrefetchScalarGridSpec(
            num_scalar_prefetch=2,
            grid=(1,),
            in_specs=[whole(a) for a in args],
            out_specs=(pl.BlockSpec(memory_space=pl.ANY),) * 11 + (whole(outs[11]),),
            scratch_shapes=[
                pltpu.VMEM((rows, width), BF),
                pltpu.VMEM((rows, width), F32),
                pltpu.VMEM((rows, width), BF),
                pltpu.VMEM((8, width, units), BF),
                pltpu.VMEM((4 * pair, width), BF),
                pltpu.VMEM((rows, width), BF),
                pltpu.VMEM((rows, width), BF),
                pltpu.VMEM((rows, 4 * units), BF),
                pltpu.VMEM((rows, 4 * units), BF),
                pltpu.SemaphoreType.DMA((3 * (rows // tile) + 8,)),
            ],
        ),
        compiler_params=params(36),
        cost_estimate=cost(31, 20_000_000),
        name="dense",
    )(ids, lengths, *args)


def input_kernel(ids, gz_ref, w_own, w_m, w_p, g0, g1, g2, g3, *rest, tile):
    out_ref = rest[-1]
    rows, width = gz_ref.shape
    pair = g0.shape[1]
    core = ids[0]

    @pl.loop(0, rows // tile)
    def _(r):
        here = place(r, tile)
        total = gz_ref[here]
        for c in range(3):
            g = jnp.concatenate([g0[c, :, here], g1[c, :, here], g2[c, :, here], g3[c, :, here]], axis=0)
            w = jnp.concatenate([w_own[c, :, place(core, pair)], w_own[c, :, place(1 - core, pair)], w_m[c], w_p[c]], axis=1)
            total = total + dot(g, w, 0, 1)
        out_ref[here] = total


def input_gradient(ids, gz, w_own, w_m, w_p, gs, waits=()):
    args = [gz, w_own, w_m, w_p, *gs]
    return pl.pallas_call(
        partial(input_kernel, tile=256),
        out_shape=jax.ShapeDtypeStruct(gz.shape, F32),
        grid_spec=pltpu.PrefetchScalarGridSpec(
            num_scalar_prefetch=1, grid=(1,),
            in_specs=[whole(a) for a in args] + [pl.BlockSpec(memory_space=pl.ANY) for _ in waits],
            out_specs=whole(gz)),
        compiler_params=params(20),
        cost_estimate=cost(7, 9_000_000),
        name="input_gradient",
    )(ids, *args, *waits)


def attention_kernel(ids, mine_near, mine_far, mate_near, mate_far, dwq_ref, dqb_ref, dwo_ref, dub_ref,
                     v0, v1, v2, v3, v4, v5, both):
    core, side = ids[0], ids[2]
    part = mine_near.shape[0]
    pair = dwo_ref.shape[0] // 2
    units = dub_ref.shape[1] // 2
    for c, near, far in ((core, mine_near, mine_far), (1 - core, mate_near, mate_far)):
        both[c, pl.ds(pl.multiple_of(side * part, 8), part)] = near[...].astype(F32)
        both[c, pl.ds(pl.multiple_of((1 - side) * part, 8), part)] = far[...].astype(F32)
    for m in range(2):
        cols = slice(m * pair, (m + 1) * pair)
        for c in range(3):
            dwq_ref[c, :, cols] = both[m, c * pair: (c + 1) * pair].T
        dwo_ref[cols] = both[m, 3 * pair: 4 * pair]
        dub_ref[:, m * units: (m + 1) * units] = both[m, 4 * pair: 4 * pair + 1]
        for c in range(2):
            dqb_ref[c: c + 1, cols] = both[m, 4 * pair + 1: 4 * pair + 2, c * pair: (c + 1) * pair]
    for k, ref in enumerate((v0, v1, v2, v3, v4, v5)):
        ref[...] = both[0, 4 * pair + 2 + k: 4 * pair + 3 + k]


def assemble_attention(ids, parts, pair, units):
    width = parts[0].shape[1]
    outs = [(3, width, 2 * pair), (2, 2 * pair), (2 * pair, width), (1, 2 * units)] + [(1, width)] * 6
    outs = tuple(jax.ShapeDtypeStruct(s, F32) for s in outs)
    return pl.pallas_call(
        attention_kernel,
        out_shape=outs,
        grid_spec=pltpu.PrefetchScalarGridSpec(
            num_scalar_prefetch=1, grid=(1,), in_specs=[whole(a) for a in parts],
            out_specs=tuple(whole(a) for a in outs),
            scratch_shapes=[pltpu.VMEM((2, 2 * parts[0].shape[0], width), F32)]),
        compiler_params=params(16),
        cost_estimate=cost(3, 4_000_000),
        name="assemble_attention",
    )(ids, *parts)


def dense_out_kernel(ids, mine_near, mine_far, mate_near, mate_far, dwu_ref, dwd_ref):
    core, side = ids[0], ids[2]
    units = mine_near.shape[1]
    part = mine_near.shape[0] // 2
    width = dwu_ref.shape[0]
    for c, near, far in ((core, mine_near, mine_far), (1 - core, mate_near, mate_far)):
        for s, ref in ((side, near), (1 - side, far)):
            dwu_ref[place(s, part), place(c, units)] = ref[:part].astype(F32)
            dwd_ref[pl.ds(pl.multiple_of(c * width + s * part, part), part)] = ref[part:].astype(F32)


def assemble_dense(ids, parts, units):
    width = parts[0].shape[1]
    outs = tuple(jax.ShapeDtypeStruct(s, F32) for s in ((width, 2 * units), (2 * units, width)))
    return pl.pallas_call(
        dense_out_kernel,
        out_shape=outs,
        grid_spec=pltpu.PrefetchScalarGridSpec(
            num_scalar_prefetch=1, grid=(1,), in_specs=[whole(a) for a in parts],
            out_specs=tuple(whole(a) for a in outs)),
        compiler_params=params(20),
        cost_estimate=cost(3, 6_000_000),
        name="assemble_dense",
    )(ids, *parts)


def cut_kernel(ids, wq, wu, wd, wo, q_out, u_out, rest_out, ids_out):
    for n in range(3):
        ids_out[n] = ids[n]
    q_out[...] = wq[...]
    u_out[...] = wu[...]
    rest_out[: wd.shape[0]] = wd[...]
    rest_out[wd.shape[0]:] = wo[...]


def cut_weights(ids, wq, wu, wd, wo):
    shapes = [(3, wq.shape[1] // 2, wq.shape[2] // 2), (wu.shape[0] // 2, wu.shape[1] // 2),
              (wd.shape[0] // 4, wd.shape[1]), (wo.shape[0] // 4, wo.shape[1])]
    spots = [lambda i, s: (0, s[2], s[0]), lambda i, s: (s[2], s[0]),
             lambda i, s: (2 * s[0] + s[2], 0), lambda i, s: (2 * s[0] + s[2], 0)]
    both = (shapes[2][0] + shapes[3][0], shapes[2][1])
    outs = [jax.ShapeDtypeStruct(a, BF) for a in (*shapes[:2], both)]
    return pl.pallas_call(
        cut_kernel,
        out_shape=(*outs, jax.ShapeDtypeStruct(ids.shape, jnp.int32)),
        grid_spec=pltpu.PrefetchScalarGridSpec(
            num_scalar_prefetch=1, grid=(1,),
            in_specs=[pl.BlockSpec(a, spot) for a, spot in zip(shapes, spots)],
            out_specs=(*[whole(a) for a in outs], pl.BlockSpec(memory_space=pltpu.SMEM))),
        compiler_params=params(8),
        cost_estimate=cost(1, 2_000_000),
        name="cut_weights",
    )(ids, *[pltpu.with_memory_space_constraint(a, pltpu.HBM) for a in (wq, wu, wd, wo)])


def send_tensor(a):
    n = lax.axis_size("tensor")
    return lax.ppermute(a, "tensor", [(i, (i + 1) % n) for i in range(n)])


def send_bit(a, bit):
    return lax.ppermute(a, "dp", [(i, i ^ (1 << bit)) for i in range(lax.axis_size("dp"))])


def plus(*members):
    return sum(m.astype(F32) for m in members).astype(BF)


def tie(*arrays):
    return lax.optimization_barrier(arrays)


def half_of(a, side, axis=0):
    n = a.shape[axis] // 2
    return lax.dynamic_slice_in_dim(a, side * n, n, axis)


def joined(mine, got, side, axis=0):
    return jnp.concatenate([jnp.where(side == 0, mine, got), jnp.where(side == 0, got, mine)], axis=axis)


def local(hidden_in, w_qkv, qv_bias, w_out, out_bias, gain1, shift1, w_up, up_bias, w_down,
          down_bias, gain2, shift2, lengths, head_perm, cotangent):
    rows, width = hidden_in.shape
    me = lax.axis_index("dp")
    core, xside, zside = me & 1, (me >> 1) & 1, (me >> 2) & 1
    upper_bits = list(range(3, lax.axis_size("dp").bit_length() - 1))
    pair = w_qkv.shape[2] // 2
    heads = head_perm.shape[0] // 2
    units = up_bias.shape[0] // 2
    row = lambda v: v.reshape(1, -1)
    ids = jnp.stack([core, lax.axis_index("tensor"), xside])

    def forward(slot, w, bias, waits=()):
        return attend_forward(ids, lengths, head_perm if slot < 2 else perm_other, hidden_in, w, bias, slot, heads, pair, waits)

    perm_other, bias_other, ub_other = send_tensor(head_perm), send_tensor(qv_bias), send_tensor(up_bias)
    *pieces, ids = cut_weights(ids, w_qkv, w_up, w_down, w_out)
    *pieces, perm_other, bias_other, ub_other = tie(*pieces, perm_other, bias_other, ub_other)
    wq_m, wu_m, rest_m = (send_tensor(a) for a in pieces)
    kept = [forward(0, w_qkv, qv_bias)]
    wq_m, ctx = tie(wq_m, kept[0][3])
    wq_got = send_bit(wq_m, 1)
    kept.append(forward(1, w_qkv, qv_bias))
    wq_got, wu_m, ctx1 = tie(wq_got, wu_m, kept[1][3])
    wu_got = send_bit(wu_m, 1)
    wq_m = joined(wq_m, wq_got, xside, 1)
    wq_p = send_bit(wq_m, 0)
    kept.append(forward(2, wq_m, bias_other))
    rest_m, wu_got, ctx2 = tie(rest_m, wu_got, kept[2][3])
    rest_got = send_bit(rest_m, 1)
    wu_m = joined(wu_m, wu_got, xside)
    wu_p = send_bit(wu_m, 0)
    kept.append(forward(3, wq_p, bias_other))
    rest_got, wu_p, ctx3 = tie(rest_got, wu_p, kept[3][3])
    wd_rows = w_down.shape[0] // 4
    wd_m = joined(rest_m[:wd_rows], rest_got[:wd_rows], xside)
    wo_m = joined(rest_m[wd_rows:], rest_got[wd_rows:], xside)
    ctxs = [ctx, ctx1, ctx2, ctx3]
    wo_p, wd_p = send_bit(wo_m, 0), send_bit(wd_m, 0)
    out, g_z1, g_attn, *ffn, smalls = dense(
        ids, lengths, hidden_in, cotangent, ctxs,
        [row(v) for v in (out_bias, gain1, shift1, down_bias, gain2, shift2)],
        [w_out, w_up, w_down, row(up_bias)], [wo_m, wu_m, wd_m, row(ub_other), wo_p, wu_p, wd_p])

    def backward(k, waits=()):
        if k < 2:
            perm, wo, block = head_perm, w_out, lambda c: c ^ k
        else:
            perm, wo, block = perm_other, (wo_m, wo_p)[k - 2], lambda c: 0
        return attend_backward(ids, perm, hidden_in, wo, block, kept[k], g_attn, smalls, k, waits)

    crossed = {n: send_bit(ffn[n], 0) for n in (6, 7, 3, 2)}
    up = [(ffn[4 * t], crossed[4 * t + 2]) for t in range(2)]
    down = [(ffn[4 * t + 1], crossed[4 * t + 3]) for t in range(2)]
    up_other = plus(*up[1])
    up_got = send_tensor(up_other)
    down_away = jnp.stack([plus(*[half_of(v, 1 - xside) for v in down[t]]) for t in range(2)])
    down_got = send_bit(down_away, 1)
    g3, d3 = backward(3, (up_other, down_away))
    d3_got = send_bit(d3, 0)
    g2, d2 = backward(2, (d3,))
    d2, up_got, down_got = tie(d2, up_got, down_got)
    up_away = plus(*[half_of(v, 1 - xside) for v in (*up[0], up_got)])
    down_other = plus(*[half_of(v, xside) for v in down[1]], down_got[1])
    up_got2 = send_bit(up_away, 1)
    down_got2 = send_tensor(down_other)
    other_away = plus(*[half_of(v, 1 - xside) for v in (d2, d3_got)])
    other_got = send_bit(other_away, 1)
    g1, d1 = backward(1, (up_away, down_other, other_away))
    d1_got = send_bit(d1, 0)
    d1, up_got2, down_got2 = tie(d1, up_got2, down_got2)
    ffn = jnp.concatenate([
        plus(*[half_of(v, xside) for v in (*up[0], up_got)], up_got2),
        plus(*[half_of(v, xside) for v in down[0]], down_got[0], down_got2)], axis=0)
    ffn_away = half_of(ffn, 1 - zside)
    ffn_got3 = send_bit(ffn_away, 2)
    ffn_away, other_got = tie(ffn_away, other_got)
    att_other = plus(*[half_of(v, xside) for v in (d2, d3_got)], other_got)
    att_got = send_tensor(att_other)
    g0, d0 = backward(0, (ffn_away, att_other))
    d0, ffn_got3 = tie(d0, ffn_got3)
    ffn = plus(half_of(ffn, zside), ffn_got3)
    d0, ffn = tie(d0, ffn)
    att_away = plus(*[half_of(v, 1 - xside) for v in (d0, d1_got)])
    att_got2 = send_bit(att_away, 1)
    ffn_got4 = [send_bit(ffn, bit) for bit in upper_bits[:1]]
    ffn, att_got, att_got2 = tie(ffn, att_got, att_got2)
    att = plus(*[half_of(v, xside) for v in (d0, d1_got)], att_got, att_got2)
    att_got3 = send_bit(half_of(att, 1 - zside), 2)
    ffn = plus(ffn, *ffn_got4)
    for bit in upper_bits[1:]:
        ffn = plus(ffn, send_bit(ffn, bit))
    ffn_got5 = send_bit(ffn, 2)
    ffn, att_got3 = tie(ffn, att_got3)
    att = plus(half_of(att, zside), att_got3)
    att_got4 = [send_bit(att, bit) for bit in upper_bits[:1]]
    att, ffn_got5 = tie(att, ffn_got5)
    ffn = joined(ffn, ffn_got5, zside)
    ffn, *att_got4 = tie(ffn, *att_got4)
    att = plus(att, *att_got4)
    for bit in upper_bits[1:]:
        att = plus(att, send_bit(att, bit))
    att = joined(att, send_bit(att, 2), zside)
    ffn_far = send_bit(ffn, 1)
    att_far = send_bit(att, 1)
    x_grad = input_gradient(ids, g_z1, w_qkv, wq_m, wq_p, [g0, g1, g2, g3], (ffn, att))
    x_grad, ffn_far = tie(x_grad, ffn_far)
    d_wu, d_wd = assemble_dense(ids, [ffn, ffn_far, send_bit(ffn, 0), send_bit(ffn_far, 0)], units)
    d_wu, att_far = tie(d_wu, att_far)
    d_wq, d_qb, d_wo, d_ub, *vecs = assemble_attention(
        ids, [att, att_far, send_bit(att, 0), send_bit(att_far, 0)], pair, units)
    v = [a.reshape(-1) for a in vecs]
    return (out, x_grad, d_wq, d_qb, d_wo, v[0], v[1], v[2], d_wu, d_ub.reshape(-1), d_wd, v[3], v[4], v[5])


def solution(mesh):
    every = P()
    rows = P(("dp", "tensor"), None)
    return jax.shard_map(
        local,
        mesh=mesh,
        in_specs=(rows, P(None, None, "tensor"), P(None, "tensor"), P("tensor", None), every, every, every,
                  P(None, "tensor"), P("tensor"), P("tensor", None), every, every, every, P("dp"), P("tensor"), rows),
        out_specs=(rows, rows, P(None, None, "tensor"), P(None, "tensor"), P("tensor", None), every, every, every,
                   P(None, "tensor"), P("tensor"), P("tensor", None), every, every, every),
        check_vma=False,
    )
```
